256 devices in a mesh: tm: 32 (over z_hi, x, core), space: 8 (over z_lo, y).
Axes of the slice: x: 4, y: 4, z: 8 (z_hi: 4, z_lo: 2; z = z_hi * 2 + z_lo), core: 2. Of those that a mesh axis runs over, the one named last changes fastest.
Arguments:
- initial: float32 [4, 65536], P(None, 'space'), may hold values from -6 to 6
- sources: float32 [32, 4, 65536], P('tm', None, 'space'), may hold values from -6 to 6
- operator: bfloat16 [128, 4, 512, 512], P('space'), may hold values from -0.015625 to 0.015625
- col_blocks: int32 [128, 4], P('space'), may hold values from 0 to 127, as said below
- coarse_inv: float32 [128, 512, 512], P('space'), may hold values from -0.5 to 0.8
Outputs:
- ends: float32 [32, 4, 65536], P('tm', None, 'space')
The draws below stay inside these ranges and needn't reach their ends.
Inputs may be any that keep to these rules, and one draw needn't show every extreme that they name: `col_blocks`: block row r lists block r, blocks r - 1 and r + 1, and one of r - 2 and r + 2, all modulo 128, in a drawn order.
All inputs are finite; a program needn't handle non-finite values.
Results may differ from the reference program's by a relative error of at most 0.00058.
Values may be sent and summed in bfloat16 or wider, within the bound.
A program may use at most 256 MiB of HBM per device.

```python
import math
import jax
import jax.numpy as jnp
from jax import lax

TRACERS = 4
BLK = 512
NNZ = 4
FINE_STEPS = 8
SLICES = 32
NB = 128
CELLS = 65536


def draw_col_blocks(key, part):
    key = jax.random.fold_in(key, 11)
    sign_key, order_key = jax.random.split(key)
    signs = jax.random.randint(sign_key, (NB,), 0, 2) * 4 - 2
    zeros = jnp.zeros((NB,), jnp.int32)
    ones = jnp.ones((NB,), jnp.int32)
    offsets = jnp.stack([zeros, zeros - ones, ones, signs.astype(jnp.int32)], axis=1)
    row_keys = jax.random.split(order_key, NB)
    orders = jax.vmap(lambda row_key: jax.random.permutation(row_key, NNZ))(row_keys)
    shuffled = jnp.take_along_axis(offsets, orders.astype(jnp.int32), axis=1)
    row_index = jnp.arange(NB, dtype=jnp.int32)[:, None]
    return jnp.mod(row_index + shuffled, NB).astype(jnp.int32)


def draw_coarse_inv(key, part):
    key = jax.random.fold_in(key, 23)
    diag_key, off_key = jax.random.split(key)
    diagonal = jax.random.uniform(diag_key, (NB, BLK), jnp.float32, 0.5, 0.75)
    offdiag = jax.random.normal(off_key, (NB, BLK, BLK), jnp.float32) * (0.2 / math.sqrt(BLK))
    identity = jnp.eye(BLK, dtype=jnp.float32)
    return offdiag * (1.0 - identity) + identity * diagonal[:, None, :]


def shard_levels(stream_key, dims, cuts, least, top_value):
    loudness, own = 1.0, jax.random.fold_in(stream_key, 6)
    for position, parts in cuts:
        draws = jnp.exp(jax.random.uniform(jax.random.fold_in(own, position), (parts,), jnp.float32, least / len(cuts), top_value / len(cuts)))
        loudness = loudness * jnp.repeat(draws, dims[position] // parts).reshape([-1 if axis == position else 1 for axis in range(len(dims))])
    return loudness


def normal_values(stream_key, shape, scale, bound, pieces=(), held_as=jnp.bfloat16):
    values = jax.random.normal(stream_key, shape, jnp.float32) * scale
    if len(pieces) > 0:
        values = shard_levels(stream_key, shape, pieces, -0.22, 0.18) * values
    return jnp.clip(values, min=-bound, max=bound).astype(held_as)


def setup_inputs(seed: int = 0) -> dict:
    streams_of = jax.random.split(jax.random.key(seed), 6)
    initial = normal_values(streams_of[0], (TRACERS, CELLS), 1.0, 6.0, ((1, 8),), jnp.float32)
    sources = normal_values(streams_of[1], (SLICES, TRACERS, CELLS), 1.0, 6.0, ((0, 32), (2, 8)), jnp.float32)
    operator = normal_values(streams_of[2], (NB, NNZ, BLK, BLK), (64 * BLK * NNZ) ** -0.5, 0.015625, ((0, 8),))
    col_blocks = draw_col_blocks(jax.random.fold_in(streams_of[5], 71), 0)
    coarse_inv = draw_coarse_inv(jax.random.fold_in(streams_of[5], 71), 0)
    return dict(initial=initial, sources=sources, operator=operator, col_blocks=col_blocks, coarse_inv=coarse_inv)


def coarse_apply(matrix, current):
    tracer_count = current.shape[0]
    stacked = current.reshape(tracer_count, NB, BLK)
    result = jnp.einsum("rab,trb->tra", matrix, stacked, precision=lax.Precision.HIGHEST)
    return result.reshape(tracer_count, NB * BLK)


def fine_step(current, wide_operator, col_blocks, forcing_share):
    rounded = current.astype(jnp.bfloat16).reshape(TRACERS, NB, BLK)
    picked = jnp.take(rounded, col_blocks, axis=1).astype(jnp.float32)
    change = jnp.einsum("rjab,trjb->tra", wide_operator, picked, precision=lax.Precision.HIGHEST)
    return current + change.reshape(TRACERS, NB * BLK) + forcing_share


def coarse_sweep(initial, increments, coarse_inv):
    def advance(anchor, increment):
        finish = coarse_apply(coarse_inv, anchor) + increment
        return finish, (anchor, finish)

    unused_last, (anchors, finishes) = lax.scan(advance, initial, increments)
    return anchors, finishes


def reference(initial, sources, operator, col_blocks, coarse_inv):
    forced = lax.map(lambda forcing: coarse_apply(coarse_inv, forcing), sources)
    anchors, unused_ends = coarse_sweep(initial, forced, coarse_inv)
    wide_operator = operator.astype(jnp.float32)

    def propagate(paired):
        anchor, forcing = paired
        forcing_share = forcing / FINE_STEPS
        current = anchor
        for repeat in range(FINE_STEPS):
            current = fine_step(current, wide_operator, col_blocks, forcing_share)
        return current - coarse_apply(coarse_inv, anchor)

    jumps = lax.map(propagate, (anchors, sources))
    unused_anchors, finishes = coarse_sweep(initial, jumps, coarse_inv)
    return finishes
```

```python
import functools

import jax
import jax.numpy as jnp
from jax import lax
from jax.experimental import pallas as pl
from jax.experimental.pallas import tpu as pltpu
from jax.sharding import PartitionSpec as P

MESH = pl.DeviceIdType.MESH
F32 = jnp.float32
BF16 = jnp.bfloat16

TRACERS = 4
BLK = 512
SLICES = 32
STEPS = 8
ROWS = 4
PAIR = 2
PIECE = PAIR * BLK
LANES = 128
LINES = PIECE // LANES
LEVELS = 4
CHUNK = 8


def slab_x(s, k):
    odd = lax.rem(s, 2)
    return 3 * odd + (1 - 2 * odd) * k


def dot(a, b):
    return jnp.dot(a, b, preferred_element_type=F32)


def halves(x):
    high = x.astype(BF16)
    return high, (x - high.astype(F32)).astype(BF16)


def kernel(
    initial_ref, sources_ref, operator_ref, cols_ref, coarse_ref, out_ref,
    coarse_vm, op_vm, opt_vm, high_vm, low_vm, init_vm, send_vm, recv_vm, osend_vm, orecv_vm,
    src_vm, v_vm, back_vm, end_vm, w_vm, halo_vm,
    load_sem, a2a_sem, hand_sem, send_sem, recv_sem,
):
    tm = lax.axis_index("tm")
    s = lax.axis_index("space")
    tracer = tm // 8
    x = lax.rem(tm // 2, 4)
    core = lax.rem(tm, 2)
    slab = slab_x(s, x)
    q = 2 * slab + core

    loads = [
        pltpu.make_async_copy(coarse_ref.at[pl.ds(ROWS * slab + PAIR * core, PAIR)], coarse_vm, load_sem.at[0]),
        pltpu.make_async_copy(
            initial_ref.at[:, pl.ds(pl.multiple_of(q * PIECE, PIECE), PIECE)], init_vm, load_sem.at[1]
        ),
        pltpu.make_async_copy(operator_ref.at[pl.ds(ROWS * slab, ROWS)], op_vm, load_sem.at[2]),
    ]
    for load in loads:
        load.start()

    barrier = pltpu.get_barrier_semaphore()

    def greet(j, carry):
        pl.semaphore_signal(barrier, inc=1, device_id=(lax.rem(tm + j, 32), s), device_id_type=MESH)
        return carry

    lax.fori_loop(1, 32, greet, 0)
    place = 4 * s + slab
    beside = []
    for step in (-1, 1):
        other = lax.rem(place + step + 32, 32)
        other_s = other // 4
        other_x = slab_x(other_s, lax.rem(other, 4))
        beside.append(((tracer * 4 + other_x) * 2 + 1, other_s))

    @pl.when(core == 1)
    def _():
        for other in beside:
            pl.semaphore_signal(barrier, inc=1, device_id=other, device_id_type=MESH)

    for piece in range(8):
        for line in range(LINES):
            at = piece * PIECE + line * LANES
            send_vm[4 * piece : 4 * piece + 4, line, :] = sources_ref[0, :, at : at + LANES]

    pl.semaphore_wait(barrier, 31 + 2 * core)

    def scatter(j, carry):
        to = lax.rem(tm + j, 32)
        to_q = 2 * slab_x(s, lax.rem(to // 2, 4)) + lax.rem(to, 2)
        pltpu.make_async_remote_copy(
            send_vm.at[to_q * 4 + to // 8], recv_vm.at[tm], a2a_sem.at[0], a2a_sem.at[1],
            device_id=(to, s), device_id_type=MESH,
        ).start()
        return carry

    lax.fori_loop(1, 32, scatter, 0)
    recv_vm[tm] = send_vm[q * 4 + tracer]

    loads[0].wait()
    for b in range(PAIR):
        high, low = halves(coarse_vm[b].T)
        high_vm[0, b] = high
        low_vm[0, b] = low

    def square(i, carry):
        level, b = i // PAIR, lax.rem(i, PAIR)
        high, low = high_vm[level, b], low_vm[level, b]
        high, low = halves(dot(high, high) + dot(high, low) + dot(low, high))
        high_vm[level + 1, b] = high
        low_vm[level + 1, b] = low
        return carry

    lax.fori_loop(0, PAIR * (LEVELS - 1), square, 0)

    loads[2].wait()

    def offset_of(i, j):
        row = ROWS * slab + i
        return lax.rem(cols_ref[row, j] - (16 * s + row) + 256, 128)

    def turn(i, carry):
        offsets = [offset_of(i, j) for j in range(4)]
        for slot in range(4):
            j = 0
            for other in range(1, 4):
                off = offsets[other]
                hit = off == (0, 127, 1)[slot] if slot < 3 else jnp.logical_or(off == 2, off == 126)
                j = jnp.where(hit, other, j)
            opt_vm[i, slot] = op_vm[i, j].T
        return carry

    lax.fori_loop(0, ROWS, turn, 0)

    def ahead(i):
        found = [(offset_of(i, j) == 2).astype(jnp.int32) for j in range(4)]
        return (found[0] + found[1] + found[2] + found[3]) > 0

    def all_pieces():
        return pltpu.make_async_remote_copy(
            send_vm.at[pl.ds(0, 31)], recv_vm.at[pl.ds(0, 31)], a2a_sem.at[0], a2a_sem.at[1],
            device_id=(tm, s), device_id_type=MESH,
        )

    loads[1].wait()
    all_pieces().wait_recv()
    all_pieces().wait_send()

    def coarse(level, value, b):
        rows = value.shape[0]
        high, low = value.astype(BF16).astype(F32), value
        both = jnp.concatenate([high, low - high], axis=0).astype(BF16)
        got = dot(both, high_vm[level, b]) + dot(both, low_vm[level, b])
        return got[:rows] + got[rows:]

    def scan(values, finish):
        for level in range(LEVELS - 1):
            by = 1 << level
            moved = [coarse(level, value, b) for b, value in enumerate(values)]
            values = [
                value + jnp.concatenate([jnp.zeros((by, BLK), F32), move[: SLICES - by]], axis=0)
                for value, move in zip(values, moved)
            ]
        last = [value[:CHUNK] for value in values]
        finish(0, last)
        for chunk in range(1, SLICES // CHUNK):
            last = [
                value[CHUNK * chunk : CHUNK * (chunk + 1)] + coarse(LEVELS - 1, before, b)
                for b, (value, before) in enumerate(zip(values, last))
            ]
            finish(chunk, last)

    first_row = lax.broadcasted_iota(jnp.int32, (SLICES, BLK), 0) == 0
    forced = []
    for b in range(PAIR):
        source = jnp.concatenate([recv_vm[:, 4 * b + line, :] for line in range(4)], axis=1)
        src_vm[PAIR * core + b] = source * (1.0 / STEPS)
        start = init_vm[pl.ds(tracer, 1), BLK * b : BLK * (b + 1)]
        forced.append(coarse(0, source + jnp.where(first_row, start, 0.0), b))

    def keep_end(chunk, last):
        for b in range(PAIR):
            end_vm[b, CHUNK * chunk : CHUNK * (chunk + 1)] = last[b]

    scan(forced, keep_end)
    for b in range(PAIR):
        start = init_vm[pl.ds(tracer, 1), BLK * b : BLK * (b + 1)]
        v_vm[PAIR * core + b] = jnp.concatenate([start, end_vm[b, : SLICES - 1]], axis=0)

    def hand(what, ref, to):
        return pltpu.make_async_remote_copy(
            ref.at[pl.ds(0, PAIR)], (v_vm, src_vm, back_vm)[what].at[pl.ds(0, PAIR)], hand_sem.at[what, 0], hand_sem.at[what, 1],
            device_id=(tm - core + to, s), device_id_type=MESH,
        )

    @pl.when(core == 0)
    def _():
        hand(0, v_vm, 1).start()
        hand(1, src_vm, 1).start()
        hand(0, v_vm, 1).wait_send()
        hand(1, src_vm, 1).wait_send()
        hand(2, v_vm, 1).wait_recv()

    @pl.when(core == 1)
    def _():
        hand(0, v_vm, 0).wait_recv()
        hand(1, src_vm, 0).wait_recv()

        def halo(parity, what):
            row = (0, 3, 1, 2)[what]
            return pltpu.make_async_remote_copy(
                w_vm.at[parity, row], halo_vm.at[parity, what], send_sem.at[parity, what],
                recv_sem.at[parity, what], device_id=beside[what % 2], device_id_type=MESH,
            )

        for row in (0, 3, 1, 2):
            w_vm[0, row] = v_vm[row].astype(BF16)
        for what in range(4):
            halo(0, what).start()
        signs = [ahead(i) for i in range(ROWS)]

        def fine(i, carry):
            now = lax.rem(i, 2)
            later = 1 - now
            w = [w_vm[now, row] for row in range(ROWS)]
            change = [
                dot(w[0], opt_vm[0, 0]) + dot(w[1], opt_vm[0, 2]),
                dot(w[0], opt_vm[1, 1]) + dot(w[1], opt_vm[1, 0]) + dot(w[2], opt_vm[1, 2]),
                dot(w[1], opt_vm[2, 1]) + dot(w[2], opt_vm[2, 0]) + dot(w[3], opt_vm[2, 2]),
                dot(w[2], opt_vm[3, 1]) + dot(w[3], opt_vm[3, 0]),
            ]

            @pl.when(i > 0)
            def _():
                for what in range(4):
                    halo(later, what).wait_send()

            halo(now, 1).wait_recv()
            left = halo_vm[now, 1]
            change[0] += dot(left, opt_vm[0, 1])
            halo(now, 0).wait_recv()
            right = halo_vm[now, 0]
            change[3] += dot(right, opt_vm[3, 2])
            halo(now, 3).wait_recv()
            change[0] += dot(jnp.where(signs[0], w[2], halo_vm[now, 3]), opt_vm[0, 3])
            halo(now, 2).wait_recv()
            change[3] += dot(jnp.where(signs[3], halo_vm[now, 2], w[1]), opt_vm[3, 3])
            for row in (0, 3):
                value = (v_vm[row] + change[row]) + src_vm[row]
                v_vm[row] = value
                w_vm[later, row] = value.astype(BF16)

            @pl.when(i < STEPS - 1)
            def _():
                halo(later, 0).start()
                halo(later, 1).start()

            change[1] += dot(jnp.where(signs[1], w[3], left), opt_vm[1, 3])
            change[2] += dot(jnp.where(signs[2], right, w[0]), opt_vm[2, 3])
            for row in (1, 2):
                value = (v_vm[row] + change[row]) + src_vm[row]
                v_vm[row] = value
                w_vm[later, row] = value.astype(BF16)

            @pl.when(i < STEPS - 1)
            def _():
                halo(later, 2).start()
                halo(later, 3).start()

            return carry

        lax.fori_loop(0, STEPS, fine, 0)
        for what in range(4):
            halo((STEPS - 1) % 2, what).wait_send()
        hand(2, v_vm, 0).start()
        hand(2, v_vm, 0).wait_send()

    def send_out(chunk, last):
        for b in range(PAIR):
            ends = end_vm[b, CHUNK * chunk : CHUNK * (chunk + 1)] + last[b]
            for line in range(4):
                osend_vm[CHUNK * chunk : CHUNK * (chunk + 1), 4 * b + line, :] = ends[:, LANES * line : LANES * (line + 1)]

        def one(j, carry):
            to = CHUNK * chunk + j

            @pl.when(to != tm)
            def _():
                pltpu.make_async_remote_copy(
                    osend_vm.at[to], orecv_vm.at[q * 4 + tracer], a2a_sem.at[2], a2a_sem.at[3],
                    device_id=(to, s), device_id_type=MESH,
                ).start()

            return carry

        lax.fori_loop(0, CHUNK, one, 0)

    scan([jnp.where(core == 0, back_vm[b], v_vm[PAIR + b]) - end_vm[b] for b in range(PAIR)], send_out)
    orecv_vm[q * 4 + tracer] = osend_vm[tm]
    back = pltpu.make_async_remote_copy(
        osend_vm.at[pl.ds(0, 31)], orecv_vm.at[pl.ds(0, 31)], a2a_sem.at[2], a2a_sem.at[3],
        device_id=(tm, s), device_id_type=MESH,
    )
    back.wait_recv()
    for piece in range(8):
        for line in range(LINES):
            at = piece * PIECE + line * LANES
            out_ref[0, :, at : at + LANES] = orecv_vm[4 * piece : 4 * piece + 4, line, :]
    back.wait_send()


def local(initial, sources, operator, col_blocks, coarse_inv):
    cells = initial.shape[1]
    return pl.pallas_call(
        kernel,
        out_shape=jax.ShapeDtypeStruct((1, TRACERS, cells), F32),
        in_specs=[
            pl.BlockSpec(memory_space=pl.ANY),
            pl.BlockSpec(memory_space=pltpu.VMEM),
            pl.BlockSpec(memory_space=pl.ANY),
            pl.BlockSpec(memory_space=pltpu.SMEM),
            pl.BlockSpec(memory_space=pl.ANY),
        ],
        out_specs=pl.BlockSpec(memory_space=pltpu.VMEM),
        scratch_shapes=[
            pltpu.VMEM((PAIR, BLK, BLK), F32),
            pltpu.VMEM((ROWS, 4, BLK, BLK), BF16),
            pltpu.VMEM((ROWS, 4, BLK, BLK), BF16),
            pltpu.VMEM((LEVELS, PAIR, BLK, BLK), BF16),
            pltpu.VMEM((LEVELS, PAIR, BLK, BLK), BF16),
            pltpu.VMEM((TRACERS, PIECE), F32),
            pltpu.VMEM((SLICES, LINES, LANES), F32),
            pltpu.VMEM((SLICES, LINES, LANES), F32),
            pltpu.VMEM((SLICES, LINES, LANES), F32),
            pltpu.VMEM((SLICES, LINES, LANES), F32),
            pltpu.VMEM((ROWS, SLICES, BLK), F32),
            pltpu.VMEM((ROWS, SLICES, BLK), F32),
            pltpu.VMEM((PAIR, SLICES, BLK), F32),
            pltpu.VMEM((PAIR, SLICES, BLK), F32),
            pltpu.VMEM((2, ROWS, SLICES, BLK), BF16),
            pltpu.VMEM((2, ROWS, SLICES, BLK), BF16),
            pltpu.SemaphoreType.DMA((3,)),
            pltpu.SemaphoreType.DMA((4,)),
            pltpu.SemaphoreType.DMA((3, 2)),
            pltpu.SemaphoreType.DMA((2, 4)),
            pltpu.SemaphoreType.DMA((2, 4)),
        ],
        compiler_params=pltpu.CompilerParams(
            collective_id=0, has_side_effects=True, vmem_limit_bytes=50 << 20
        ),
        name="parareal",
    )(initial, sources, operator, col_blocks, coarse_inv)


def solution(mesh):
    placed = (
        P(None, "space"),
        P("tm", None, "space"),
        P("space", None, None, None),
        P("space", None),
        P("space", None, None),
    )
    return jax.shard_map(
        local, mesh=mesh, in_specs=placed, out_specs=P("tm", None, "space"), check_vma=False
    )
```

```python
import jax
import jax.numpy as jnp
from jax import lax
from jax.experimental import pallas as pl
from jax.experimental.pallas import tpu as pltpu
from jax.sharding import PartitionSpec as P

MESH = pl.DeviceIdType.MESH
F32 = jnp.float32
BF16 = jnp.bfloat16

TRACERS = 4
BLK = 512
SLICES = 32
STEPS = 8
ROWS = 4
PAIR = 2
PIECE = PAIR * BLK
LANES = 128
LINES = PIECE // LANES
LEVELS = 4
CHUNK = 8
PART = 16
PARTS = SLICES // PART


def slab_x(s, k):
    odd = lax.rem(s, 2)
    return 3 * odd + (1 - 2 * odd) * k


def dot(a, b):
    return jnp.dot(a, b, preferred_element_type=F32)


def halves(x):
    high = x.astype(BF16)
    return high, (x - high.astype(F32)).astype(BF16)


def kernel(
    initial_ref, sources_ref, operator_ref, cols_ref, coarse_ref, out_ref,
    source_vm, cols_sm, coarse_vm, op_vm, opt_vm, high_vm, low_vm, init_vm, send_vm, recv_vm, osend_vm, orecv_vm,
    src_vm, v_vm, back_vm, end_vm, w_vm, halo_vm,
    load_sem, a2a_sem, hand_sem, send_sem, recv_sem,
):
    tm = lax.axis_index("tm")
    s = lax.axis_index("space")
    tracer = tm // 8
    inner = lax.rem(tm, 8)
    x = inner // 2
    core = lax.rem(tm, 2)
    slab = slab_x(s, x)
    q = 2 * slab + core

    barrier = pltpu.get_barrier_semaphore()

    def others(do):
        for away in (2, 1, 3, 0):
            base = 8 * lax.rem(tracer + away, 4)

            def one(j, carry):
                do(base + lax.rem(inner + j, 8))
                return carry

            lax.fori_loop(1 if away == 0 else 0, 8, one, 0)

    def greet(to):
        pl.semaphore_signal(barrier, inc=1, device_id=to, device_id_type=MESH)

    place = 4 * s + slab
    beside = []
    for step in (-1, 1):
        other = lax.rem(place + step + 32, 32)
        other_s = other // 4
        other_x = slab_x(other_s, lax.rem(other, 4))
        beside.append(((tracer * 4 + other_x) * 2 + 1, other_s))

    greet(beside[0])

    @pl.when(core == 1)
    def _():
        greet(beside[1])
        greet((beside[1][0] - 1, beside[1][1]))

    others(lambda to: greet((to, s)))

    load_sources = pltpu.make_async_copy(sources_ref.at[0], source_vm, load_sem.at[0])
    load_coarse = pltpu.make_async_copy(
        coarse_ref.at[pl.ds(ROWS * slab + PAIR * core, PAIR)], coarse_vm, load_sem.at[1]
    )
    load_initial = pltpu.make_async_copy(
        initial_ref.at[:, pl.ds(pl.multiple_of(q * PIECE, PIECE), PIECE)], init_vm, load_sem.at[2]
    )
    load_cols = pltpu.make_async_copy(cols_ref, cols_sm, load_sem.at[3])
    load_operator = pltpu.make_async_copy(operator_ref.at[pl.ds(ROWS * slab, ROWS)], op_vm, load_sem.at[4])
    for load in (load_sources, load_coarse, load_initial, load_cols, load_operator):
        load.start()

    load_sources.wait()
    for piece in range(8):
        for line in range(LINES):
            at = piece * PIECE + line * LANES
            send_vm[4 * piece : 4 * piece + 4, line, :] = source_vm[:, at : at + LANES]
    recv_vm[tm] = send_vm[q * 4 + tracer]

    load_coarse.wait()
    for b in range(PAIR):
        high, low = halves(coarse_vm[b].T)
        high_vm[0, b] = high
        low_vm[0, b] = low

    def square(i):
        level, b = i // PAIR, lax.rem(i, PAIR)
        high, low = high_vm[level, b], low_vm[level, b]
        high, low = halves(dot(high, high) + dot(high, low) + dot(low, high))
        high_vm[level + 1, b] = high
        low_vm[level + 1, b] = low

    pl.semaphore_wait(barrier, 32 + 2 * core)

    def scatter(to):
        to_q = 2 * slab_x(s, lax.rem(to // 2, 4)) + lax.rem(to, 2)
        pltpu.make_async_remote_copy(
            send_vm.at[to_q * 4 + to // 8], recv_vm.at[tm], a2a_sem.at[0], a2a_sem.at[1],
            device_id=(to, s), device_id_type=MESH,
        ).start()

    others(scatter)

    load_cols.wait()
    load_operator.wait()

    def offset_of(i, j):
        row = ROWS * slab + i
        return lax.rem(cols_sm[j, row] - (16 * s + row) + 256, 128)

    def turn(i):
        offsets = [offset_of(i, j) for j in range(4)]
        for slot in range(4):
            j = 0
            for other in range(1, 4):
                off = offsets[other]
                hit = off == (0, 127, 1)[slot] if slot < 3 else jnp.logical_or(off == 2, off == 126)
                j = jnp.where(hit, other, j)
            opt_vm[i, slot] = op_vm[i, j].T

    def late(i, carry):
        square(i)
        turn(i)
        return carry

    lax.fori_loop(0, ROWS, late, 0)

    def ahead(i):
        found = [(offset_of(i, j) == 2).astype(jnp.int32) for j in range(4)]
        return (found[0] + found[1] + found[2] + found[3]) > 0

    def all_pieces():
        return pltpu.make_async_remote_copy(
            send_vm.at[pl.ds(0, 31)], recv_vm.at[pl.ds(0, 31)], a2a_sem.at[0], a2a_sem.at[1],
            device_id=(tm, s), device_id_type=MESH,
        )

    load_initial.wait()
    all_pieces().wait_recv()

    def coarse(level, value, b):
        rows = value.shape[0]
        high, low = value.astype(BF16).astype(F32), value
        both = jnp.concatenate([high, low - high], axis=0).astype(BF16)
        got = dot(both, high_vm[level, b]) + dot(both, low_vm[level, b])
        return got[:rows] + got[rows:]

    def scan(values, leap, finish):
        for level in range(LEVELS - 1):
            by = 1 << level
            moved = [coarse(level, value, b) for b, value in enumerate(values)]
            values = [
                value + jnp.concatenate([jnp.zeros((by, BLK), F32), move[: SLICES - by]], axis=0)
                for value, move in zip(values, moved)
            ]
        last = [value[:CHUNK] for value in values]
        finish(0, last)
        for chunk in range(1, SLICES // CHUNK):
            last = [
                value[CHUNK * chunk : CHUNK * (chunk + 1)] + leap(before, b)
                for b, (value, before) in enumerate(zip(values, last))
            ]
            finish(chunk, last)

    first_row = lax.broadcasted_iota(jnp.int32, (SLICES, BLK), 0) == 0
    forced = []
    for b in range(PAIR):
        source = jnp.concatenate([recv_vm[:, 4 * b + line, :] for line in range(4)], axis=1)
        src_vm[PAIR * core + b] = source * (1.0 / STEPS)
        start = init_vm[pl.ds(tracer, 1), BLK * b : BLK * (b + 1)]
        forced.append(coarse(0, source + jnp.where(first_row, start, 0.0), b))

    def keep_end(chunk, last):
        for b in range(PAIR):
            end_vm[b, CHUNK * chunk : CHUNK * (chunk + 1)] = last[b]

    def hand(what, ref, to):
        return pltpu.make_async_remote_copy(
            ref.at[pl.ds(0, PAIR)], (v_vm, src_vm, back_vm)[what].at[pl.ds(0, PAIR)], hand_sem.at[what, 0], hand_sem.at[what, 1],
            device_id=(tm - core + to, s), device_id_type=MESH,
        )

    def halo(parity, what, part):
        rows = pl.ds(PART * part, PART)
        return pltpu.make_async_remote_copy(
            w_vm.at[parity, (0, 3, 1, 2)[what], rows], halo_vm.at[parity, what, rows], send_sem.at[parity, what, part],
            recv_sem.at[parity, what, part], device_id=beside[what % 2], device_id_type=MESH,
        )

    @pl.when(core == 0)
    def _():
        hand(1, src_vm, 1).start()

    scan(forced, lambda before, b: coarse(2, coarse(2, before, b), b), keep_end)
    for b in range(PAIR):
        start = init_vm[pl.ds(tracer, 1), BLK * b : BLK * (b + 1)]
        start = jnp.concatenate([start, end_vm[b, : SLICES - 1]], axis=0)
        v_vm[PAIR * core + b] = start
        w_vm[0, PAIR * core + b] = start.astype(BF16)

    def last_powers():
        def one(b, carry):
            square(2 * PAIR + b)
            return carry

        lax.fori_loop(0, PAIR, one, 0)

    @pl.when(core == 0)
    def _():
        for part in range(PARTS):
            halo(0, 0, part).start()
            halo(0, 2, part).start()
        hand(0, v_vm, 1).start()
        last_powers()
        for part in range(PARTS):
            halo(0, 0, part).wait_send()
            halo(0, 2, part).wait_send()
        hand(0, v_vm, 1).wait_send()
        hand(1, src_vm, 1).wait_send()
        hand(2, v_vm, 1).wait_recv()

    @pl.when(core == 1)
    def _():
        for part in range(PARTS):
            halo(0, 1, part).start()
            halo(0, 3, part).start()
        last_powers()
        hand(0, v_vm, 0).wait_recv()
        for row in range(PAIR):
            w_vm[0, row] = v_vm[row].astype(BF16)
        hand(1, src_vm, 0).wait_recv()
        signs = [ahead(i) for i in range(ROWS)]

        def fine(i, carry):
            now = lax.rem(i, 2)
            later = 1 - now
            w = [w_vm[now, row] for row in range(ROWS)]
            inside = [
                dot(w[0], opt_vm[0, 0]) + dot(w[1], opt_vm[0, 2]),
                dot(w[0], opt_vm[1, 1]) + dot(w[1], opt_vm[1, 0]) + dot(w[2], opt_vm[1, 2]),
                dot(w[1], opt_vm[2, 1]) + dot(w[2], opt_vm[2, 0]) + dot(w[3], opt_vm[2, 2]),
                dot(w[2], opt_vm[3, 1]) + dot(w[3], opt_vm[3, 0]),
            ]

            @pl.when(i > 0)
            def _():
                for part in range(PARTS):
                    halo(later, 1, part).wait_send()
                    halo(later, 3, part).wait_send()

            @pl.when(i > 1)
            def _():
                for part in range(PARTS):
                    halo(later, 0, part).wait_send()
                    halo(later, 2, part).wait_send()

            for part in range(PARTS):
                at = slice(PART * part, PART * (part + 1))
                change = [value[at] for value in inside]

                def update(row):
                    value = (v_vm[row, at] + change[row]) + src_vm[row, at]
                    v_vm[row, at] = value
                    w_vm[later, row, at] = value.astype(BF16)

                halo(now, 1, part).wait_recv()
                left = halo_vm[now, 1, at]
                change[0] += dot(left, opt_vm[0, 1])
                halo(now, 0, part).wait_recv()
                right = halo_vm[now, 0, at]
                change[3] += dot(right, opt_vm[3, 2])
                halo(now, 3, part).wait_recv()
                change[0] += dot(jnp.where(signs[0], w[2][at], halo_vm[now, 3, at]), opt_vm[0, 3])
                halo(now, 2, part).wait_recv()
                change[3] += dot(jnp.where(signs[3], halo_vm[now, 2, at], w[1][at]), opt_vm[3, 3])
                update(0)
                update(3)

                @pl.when(i < STEPS - 1)
                def _():
                    halo(later, 0, part).start()
                    halo(later, 1, part).start()

                change[1] += dot(jnp.where(signs[1], w[3][at], left), opt_vm[1, 3])
                change[2] += dot(jnp.where(signs[2], right, w[0][at]), opt_vm[2, 3])
                update(1)
                update(2)

                @pl.when(i < STEPS - 1)
                def _():
                    halo(later, 2, part).start()
                    halo(later, 3, part).start()

            return carry

        lax.fori_loop(0, STEPS, fine, 0)
        for part in range(PARTS):
            for what in range(4):
                halo((STEPS - 1) % 2, what, part).wait_send()
        hand(2, v_vm, 0).start()
        hand(2, v_vm, 0).wait_send()

    def send_out(chunk, last):
        for b in range(PAIR):
            ends = end_vm[b, CHUNK * chunk : CHUNK * (chunk + 1)] + last[b]
            for line in range(4):
                osend_vm[CHUNK * chunk : CHUNK * (chunk + 1), 4 * b + line, :] = ends[:, LANES * line : LANES * (line + 1)]

        def one(j, carry):
            to = CHUNK * chunk + lax.rem(inner + j, CHUNK)

            @pl.when(to != tm)
            def _():
                pltpu.make_async_remote_copy(
                    osend_vm.at[to], orecv_vm.at[q * 4 + tracer], a2a_sem.at[2], a2a_sem.at[3],
                    device_id=(to, s), device_id_type=MESH,
                ).start()

            return carry

        lax.fori_loop(0, CHUNK, one, 0)

    scan([jnp.where(core == 0, back_vm[b], v_vm[PAIR + b]) - end_vm[b] for b in range(PAIR)], lambda before, b: coarse(3, before, b), send_out)
    orecv_vm[q * 4 + tracer] = osend_vm[tm]
    back = pltpu.make_async_remote_copy(
        osend_vm.at[pl.ds(0, 31)], orecv_vm.at[pl.ds(0, 31)], a2a_sem.at[2], a2a_sem.at[3],
        device_id=(tm, s), device_id_type=MESH,
    )
    back.wait_recv()
    for piece in range(8):
        for line in range(LINES):
            at = piece * PIECE + line * LANES
            out_ref[0, :, at : at + LANES] = orecv_vm[4 * piece : 4 * piece + 4, line, :]
    back.wait_send()
    all_pieces().wait_send()


def local(initial, sources, operator, col_blocks, coarse_inv):
    cells = initial.shape[1]
    cols = col_blocks.T
    return pl.pallas_call(
        kernel,
        out_shape=pltpu.VMEM((1, TRACERS, cells), F32),
        in_specs=[
            pl.BlockSpec(memory_space=pltpu.HBM),
            pl.BlockSpec(memory_space=pltpu.HBM),
            pl.BlockSpec(memory_space=pltpu.HBM),
            pl.BlockSpec(memory_space=pltpu.HBM),
            pl.BlockSpec(memory_space=pltpu.HBM),
        ],
        out_specs=pl.BlockSpec(memory_space=pltpu.VMEM),
        scratch_shapes=[
            pltpu.VMEM((TRACERS, cells), F32),
            pltpu.SMEM(cols.shape, jnp.int32),
            pltpu.VMEM((PAIR, BLK, BLK), F32),
            pltpu.VMEM((ROWS, 4, BLK, BLK), BF16),
            pltpu.VMEM((ROWS, 4, BLK, BLK), BF16),
            pltpu.VMEM((LEVELS, PAIR, BLK, BLK), BF16),
            pltpu.VMEM((LEVELS, PAIR, BLK, BLK), BF16),
            pltpu.VMEM((TRACERS, PIECE), F32),
            pltpu.VMEM((SLICES, LINES, LANES), F32),
            pltpu.VMEM((SLICES, LINES, LANES), F32),
            pltpu.VMEM((SLICES, LINES, LANES), F32),
            pltpu.VMEM((SLICES, LINES, LANES), F32),
            pltpu.VMEM((ROWS, SLICES, BLK), F32),
            pltpu.VMEM((ROWS, SLICES, BLK), F32),
            pltpu.VMEM((PAIR, SLICES, BLK), F32),
            pltpu.VMEM((PAIR, SLICES, BLK), F32),
            pltpu.VMEM((2, ROWS, SLICES, BLK), BF16),
            pltpu.VMEM((2, ROWS, SLICES, BLK), BF16),
            pltpu.SemaphoreType.DMA((5,)),
            pltpu.SemaphoreType.DMA((4,)),
            pltpu.SemaphoreType.DMA((3, 2)),
            pltpu.SemaphoreType.DMA((2, 4, PARTS)),
            pltpu.SemaphoreType.DMA((2, 4, PARTS)),
        ],
        compiler_params=pltpu.CompilerParams(
            collective_id=0, has_side_effects=True, vmem_limit_bytes=63 << 20
        ),
        name="parareal",
    )(initial, sources, operator, cols, coarse_inv)


def solution(mesh):
    placed = (
        P(None, "space"),
        P("tm", None, "space"),
        P("space", None, None, None),
        P("space", None),
        P("space", None, None),
    )
    return jax.shard_map(
        local, mesh=mesh, in_specs=placed, out_specs=P("tm", None, "space"), check_vma=False
    )
```

```python
import jax
import jax.numpy as jnp
from jax import lax
from jax.experimental import pallas as pl
from jax.experimental.pallas import tpu as pltpu
from jax.sharding import PartitionSpec as P

MESH = pl.DeviceIdType.MESH
F32 = jnp.float32
BF16 = jnp.bfloat16

TRACERS = 4
BLK = 512
SLICES = 32
STEPS = 8
ROWS = 4
PAIR = 2
PIECE = PAIR * BLK
LANES = 128
LINES = PIECE // LANES
LEVELS = 4
CHUNK = 8
PART = 16
PARTS = SLICES // PART


def slab_x(s, k):
    odd = lax.rem(s, 2)
    return 3 * odd + (1 - 2 * odd) * k


def dot(a, b):
    return jnp.dot(a, b, preferred_element_type=F32)


def halves(x):
    high = x.astype(BF16)
    return high, (x - high.astype(F32)).astype(BF16)


def kernel(
    initial_ref, sources_ref, operator_ref, cols_ref, coarse_ref, out_ref,
    source_vm, cols_sm, coarse_vm, op_vm, opt_vm, high_vm, low_vm, init_vm, send_vm, recv_vm, osend_vm, orecv_vm,
    src_vm, v_vm, back_vm, end_vm, w_vm, halo_vm,
    load_sem, a2a_sem, hand_sem, send_sem, recv_sem,
):
    tm = lax.axis_index("tm")
    s = lax.axis_index("space")
    tracer = tm // 8
    inner = lax.rem(tm, 8)
    x = inner // 2
    core = lax.rem(tm, 2)
    slab = slab_x(s, x)
    q = 2 * slab + core

    barrier = pltpu.get_barrier_semaphore()

    def others(do):
        for away in (2, 1, 3, 0):
            base = 8 * lax.rem(tracer + away, 4)

            def one(j, carry):
                do(base + lax.rem(inner + j, 8))
                return carry

            lax.fori_loop(1 if away == 0 else 0, 8, one, 0)

    def greet(to):
        pl.semaphore_signal(barrier, inc=1, device_id=to, device_id_type=MESH)

    place = 4 * s + slab
    beside = []
    for step in (-1, 1):
        other = lax.rem(place + step + 32, 32)
        other_s = other // 4
        other_x = slab_x(other_s, lax.rem(other, 4))
        beside.append(((tracer * 4 + other_x) * 2 + 1, other_s))

    greet(beside[0])

    @pl.when(core == 1)
    def _():
        greet(beside[1])
        greet((beside[1][0] - 1, beside[1][1]))

    others(lambda to: greet((to, s)))

    load_sources = pltpu.make_async_copy(sources_ref.at[0], source_vm, load_sem.at[0])
    load_coarse = pltpu.make_async_copy(
        coarse_ref.at[pl.ds(ROWS * slab + PAIR * core, PAIR)], coarse_vm, load_sem.at[1]
    )
    load_initial = pltpu.make_async_copy(
        initial_ref.at[:, pl.ds(pl.multiple_of(q * PIECE, PIECE), PIECE)], init_vm, load_sem.at[2]
    )
    load_cols = pltpu.make_async_copy(cols_ref, cols_sm, load_sem.at[3])
    load_operator = pltpu.make_async_copy(operator_ref.at[pl.ds(ROWS * slab, ROWS)], op_vm, load_sem.at[4])
    for load in (load_sources, load_coarse, load_initial, load_cols, load_operator):
        load.start()

    load_sources.wait()
    for piece in range(8):
        for line in range(LINES):
            at = piece * PIECE + line * LANES
            send_vm[4 * piece : 4 * piece + 4, line, :] = source_vm[:, at : at + LANES]
    recv_vm[tm] = send_vm[q * 4 + tracer]

    load_coarse.wait()
    for b in range(PAIR):
        high, low = halves(coarse_vm[b].T)
        high_vm[0, b] = high
        low_vm[0, b] = low

    def square(i):
        level, b = i // PAIR, lax.rem(i, PAIR)
        high, low = high_vm[level, b], low_vm[level, b]
        high, low = halves(dot(high, high) + dot(high, low) + dot(low, high))
        high_vm[level + 1, b] = high
        low_vm[level + 1, b] = low

    pl.semaphore_wait(barrier, 32 + 2 * core)

    def scatter(to):
        to_q = 2 * slab_x(s, lax.rem(to // 2, 4)) + lax.rem(to, 2)
        pltpu.make_async_remote_copy(
            send_vm.at[to_q * 4 + to // 8], recv_vm.at[tm], a2a_sem.at[0], a2a_sem.at[1],
            device_id=(to, s), device_id_type=MESH,
        ).start()

    others(scatter)

    load_cols.wait()
    load_operator.wait()

    def offset_of(i, j):
        row = ROWS * slab + i
        return lax.rem(cols_sm[j, row] - (16 * s + row) + 256, 128)

    def turn(i):
        offsets = [offset_of(i, j) for j in range(4)]
        for slot in range(4):
            j = 0
            for other in range(1, 4):
                off = offsets[other]
                hit = off == (0, 127, 1)[slot] if slot < 3 else jnp.logical_or(off == 2, off == 126)
                j = jnp.where(hit, other, j)
            opt_vm[i, slot] = op_vm[i, j].T

    def late(i, carry):
        square(i)
        turn(i)
        return carry

    lax.fori_loop(0, ROWS, late, 0)

    def last(b, carry):
        square(ROWS + b)
        return carry

    lax.fori_loop(0, PAIR, last, 0)

    def ahead(i):
        found = [(offset_of(i, j) == 2).astype(jnp.int32) for j in range(4)]
        return (found[0] + found[1] + found[2] + found[3]) > 0

    def all_pieces():
        return pltpu.make_async_remote_copy(
            send_vm.at[pl.ds(0, 31)], recv_vm.at[pl.ds(0, 31)], a2a_sem.at[0], a2a_sem.at[1],
            device_id=(tm, s), device_id_type=MESH,
        )

    load_initial.wait()
    all_pieces().wait_recv()

    def coarse(level, value, b):
        rows = value.shape[0]
        high, low = value.astype(BF16).astype(F32), value
        both = jnp.concatenate([high, low - high], axis=0).astype(BF16)
        got = dot(both, high_vm[level, b]) + dot(both, low_vm[level, b])
        return got[:rows] + got[rows:]

    def scan(values, finish):
        for level in range(LEVELS - 1):
            by = 1 << level
            moved = [coarse(level, value, b) for b, value in enumerate(values)]
            values = [
                value + jnp.concatenate([jnp.zeros((by, BLK), F32), move[: SLICES - by]], axis=0)
                for value, move in zip(values, moved)
            ]
        last = [value[:CHUNK] for value in values]
        finish(0, last)
        for chunk in range(1, SLICES // CHUNK):
            last = [
                value[CHUNK * chunk : CHUNK * (chunk + 1)] + coarse(LEVELS - 1, before, b)
                for b, (value, before) in enumerate(zip(values, last))
            ]
            finish(chunk, last)

    first_row = lax.broadcasted_iota(jnp.int32, (SLICES, BLK), 0) == 0
    forced = []
    for b in range(PAIR):
        source = jnp.concatenate([recv_vm[:, 4 * b + line, :] for line in range(4)], axis=1)
        src_vm[PAIR * core + b] = source * (1.0 / STEPS)
        start = init_vm[pl.ds(tracer, 1), BLK * b : BLK * (b + 1)]
        forced.append(coarse(0, source + jnp.where(first_row, start, 0.0), b))

    def keep_end(chunk, last):
        for b in range(PAIR):
            end_vm[b, CHUNK * chunk : CHUNK * (chunk + 1)] = last[b]

    def hand(what, ref, to):
        return pltpu.make_async_remote_copy(
            ref.at[pl.ds(0, PAIR)], (v_vm, src_vm, back_vm)[what].at[pl.ds(0, PAIR)], hand_sem.at[what, 0], hand_sem.at[what, 1],
            device_id=(tm - core + to, s), device_id_type=MESH,
        )

    def halo(parity, what, part):
        rows = pl.ds(PART * part, PART)
        return pltpu.make_async_remote_copy(
            w_vm.at[parity, (0, 3, 1, 2)[what], rows], halo_vm.at[parity, what, rows], send_sem.at[parity, what, part],
            recv_sem.at[parity, what, part], device_id=beside[what % 2], device_id_type=MESH,
        )

    @pl.when(core == 0)
    def _():
        hand(1, src_vm, 1).start()

    scan(forced, keep_end)
    for b in range(PAIR):
        start = init_vm[pl.ds(tracer, 1), BLK * b : BLK * (b + 1)]
        start = jnp.concatenate([start, end_vm[b, : SLICES - 1]], axis=0)
        v_vm[PAIR * core + b] = start
        w_vm[0, PAIR * core + b] = start.astype(BF16)

    @pl.when(core == 0)
    def _():
        for part in range(PARTS):
            halo(0, 0, part).start()
            halo(0, 2, part).start()
        hand(0, v_vm, 1).start()
        for part in range(PARTS):
            halo(0, 0, part).wait_send()
            halo(0, 2, part).wait_send()
        hand(0, v_vm, 1).wait_send()
        hand(1, src_vm, 1).wait_send()
        hand(2, v_vm, 1).wait_recv()

    @pl.when(core == 1)
    def _():
        for part in range(PARTS):
            halo(0, 1, part).start()
            halo(0, 3, part).start()
        hand(0, v_vm, 0).wait_recv()
        for row in range(PAIR):
            w_vm[0, row] = v_vm[row].astype(BF16)
        hand(1, src_vm, 0).wait_recv()
        signs = [ahead(i) for i in range(ROWS)]

        def fine(i, carry):
            now = lax.rem(i, 2)
            later = 1 - now
            w = [w_vm[now, row] for row in range(ROWS)]
            inside = [
                dot(w[0], opt_vm[0, 0]) + dot(w[1], opt_vm[0, 2]),
                dot(w[0], opt_vm[1, 1]) + dot(w[1], opt_vm[1, 0]) + dot(w[2], opt_vm[1, 2]),
                dot(w[1], opt_vm[2, 1]) + dot(w[2], opt_vm[2, 0]) + dot(w[3], opt_vm[2, 2]),
                dot(w[2], opt_vm[3, 1]) + dot(w[3], opt_vm[3, 0]),
            ]

            @pl.when(i > 0)
            def _():
                for part in range(PARTS):
                    halo(later, 1, part).wait_send()
                    halo(later, 3, part).wait_send()

            @pl.when(i > 1)
            def _():
                for part in range(PARTS):
                    halo(later, 0, part).wait_send()
                    halo(later, 2, part).wait_send()

            for side in range(2):
                edge, next_in = (0, 1) if side == 0 else (3, 2)
                toward = 1 + side
                for part in range(PARTS):
                    at = slice(PART * part, PART * (part + 1))

                    def update(row, change):
                        value = (v_vm[row, at] + change) + src_vm[row, at]
                        v_vm[row, at] = value
                        w_vm[later, row, at] = value.astype(BF16)

                    def send(what):
                        @pl.when(i < STEPS - 1)
                        def _():
                            halo(later, what, part).start()

                    halo(now, 1 - side, part).wait_recv()
                    near = halo_vm[now, 1 - side, at]
                    change = inside[edge][at] + dot(near, opt_vm[edge, toward])
                    halo(now, 3 - side, part).wait_recv()
                    far = halo_vm[now, 3 - side, at]
                    out = signs[edge] if side == 1 else jnp.logical_not(signs[edge])
                    update(edge, change + dot(jnp.where(out, far, w[3 - next_in][at]), opt_vm[edge, 3]))
                    send(side)
                    out = signs[next_in] if side == 1 else jnp.logical_not(signs[next_in])
                    change = dot(jnp.where(out, near, w[3 - edge][at]), opt_vm[next_in, 3])
                    update(next_in, inside[next_in][at] + change)
                    send(2 + side)

                if side == 0:

                    @pl.when(i == STEPS - 1)
                    def _():
                        hand(2, v_vm, 0).start()

            return carry

        lax.fori_loop(0, STEPS, fine, 0)
        for part in range(PARTS):
            for what in range(4):
                halo((STEPS - 1) % 2, what, part).wait_send()
        hand(2, v_vm, 0).wait_send()

    def send_out(chunk, last):
        for b in range(PAIR):
            ends = end_vm[b, CHUNK * chunk : CHUNK * (chunk + 1)] + last[b]
            for line in range(4):
                osend_vm[CHUNK * chunk : CHUNK * (chunk + 1), 4 * b + line, :] = ends[:, LANES * line : LANES * (line + 1)]

        def one(j, carry):
            to = CHUNK * chunk + lax.rem(inner + j, CHUNK)

            @pl.when(to != tm)
            def _():
                pltpu.make_async_remote_copy(
                    osend_vm.at[to], orecv_vm.at[q * 4 + tracer], a2a_sem.at[2], a2a_sem.at[3],
                    device_id=(to, s), device_id_type=MESH,
                ).start()

            return carry

        lax.fori_loop(0, CHUNK, one, 0)

    scan([jnp.where(core == 0, back_vm[b], v_vm[PAIR + b]) - end_vm[b] for b in range(PAIR)], send_out)
    orecv_vm[q * 4 + tracer] = osend_vm[tm]
    back = pltpu.make_async_remote_copy(
        osend_vm.at[pl.ds(0, 31)], orecv_vm.at[pl.ds(0, 31)], a2a_sem.at[2], a2a_sem.at[3],
        device_id=(tm, s), device_id_type=MESH,
    )
    back.wait_recv()
    for piece in range(8):
        for line in range(LINES):
            at = piece * PIECE + line * LANES
            out_ref[0, :, at : at + LANES] = orecv_vm[4 * piece : 4 * piece + 4, line, :]
    back.wait_send()
    all_pieces().wait_send()


def local(initial, sources, operator, col_blocks, coarse_inv):
    cells = initial.shape[1]
    cols = col_blocks.T
    return pl.pallas_call(
        kernel,
        out_shape=pltpu.VMEM((1, TRACERS, cells), F32),
        in_specs=[
            pl.BlockSpec(memory_space=pltpu.HBM),
            pl.BlockSpec(memory_space=pltpu.HBM),
            pl.BlockSpec(memory_space=pltpu.HBM),
            pl.BlockSpec(memory_space=pltpu.HBM),
            pl.BlockSpec(memory_space=pltpu.HBM),
        ],
        out_specs=pl.BlockSpec(memory_space=pltpu.VMEM),
        scratch_shapes=[
            pltpu.VMEM((TRACERS, cells), F32),
            pltpu.SMEM(cols.shape, jnp.int32),
            pltpu.VMEM((PAIR, BLK, BLK), F32),
            pltpu.VMEM((ROWS, 4, BLK, BLK), BF16),
            pltpu.VMEM((ROWS, 4, BLK, BLK), BF16),
            pltpu.VMEM((LEVELS, PAIR, BLK, BLK), BF16),
            pltpu.VMEM((LEVELS, PAIR, BLK, BLK), BF16),
            pltpu.VMEM((TRACERS, PIECE), F32),
            pltpu.VMEM((SLICES, LINES, LANES), F32),
            pltpu.VMEM((SLICES, LINES, LANES), F32),
            pltpu.VMEM((SLICES, LINES, LANES), F32),
            pltpu.VMEM((SLICES, LINES, LANES), F32),
            pltpu.VMEM((ROWS, SLICES, BLK), F32),
            pltpu.VMEM((ROWS, SLICES, BLK), F32),
            pltpu.VMEM((PAIR, SLICES, BLK), F32),
            pltpu.VMEM((PAIR, SLICES, BLK), F32),
            pltpu.VMEM((2, ROWS, SLICES, BLK), BF16),
            pltpu.VMEM((2, ROWS, SLICES, BLK), BF16),
            pltpu.SemaphoreType.DMA((5,)),
            pltpu.SemaphoreType.DMA((4,)),
            pltpu.SemaphoreType.DMA((3, 2)),
            pltpu.SemaphoreType.DMA((2, 4, PARTS)),
            pltpu.SemaphoreType.DMA((2, 4, PARTS)),
        ],
        compiler_params=pltpu.CompilerParams(
            collective_id=0, has_side_effects=True, vmem_limit_bytes=63 << 20
        ),
        name="parareal",
    )(initial, sources, operator, cols, coarse_inv)


def solution(mesh):
    placed = (
        P(None, "space"),
        P("tm", None, "space"),
        P("space", None, None, None),
        P("space", None),
        P("space", None, None),
    )
    return jax.shard_map(
        local, mesh=mesh, in_specs=placed, out_specs=P("tm", None, "space"), check_vma=False
    )
```

```python
import jax
import jax.numpy as jnp
from jax import lax
from jax.experimental import pallas as pl
from jax.experimental.pallas import tpu as pltpu
from jax.sharding import PartitionSpec as P

MESH = pl.DeviceIdType.MESH
F32 = jnp.float32
BF16 = jnp.bfloat16

TRACERS = 4
BLK = 512
SLICES = 32
STEPS = 8
ROWS = 4
PAIR = 2
PIECE = PAIR * BLK
LANES = 128
LINES = PIECE // LANES
LEVELS = 4
CHUNK = 8
PART = 16
PARTS = SLICES // PART


def slab_x(s, k):
    odd = lax.rem(s, 2)
    return 3 * odd + (1 - 2 * odd) * k


def dot(a, b):
    return jnp.dot(a, b, preferred_element_type=F32)


def halves(x):
    high = x.astype(BF16)
    return high, (x - high.astype(F32)).astype(BF16)


def kernel(
    initial_ref, sources_ref, operator_ref, cols_ref, coarse_ref, out_ref,
    source_vm, cols_sm, coarse_vm, op_vm, opt_vm, high_vm, low_vm, init_vm, send_vm, recv_vm, osend_vm, orecv_vm,
    src_vm, v_vm, back_vm, end_vm, w_vm, halo_vm,
    load_sem, a2a_sem, hand_sem, send_sem, recv_sem,
):
    tm = lax.axis_index("tm")
    s = lax.axis_index("space")
    tracer = tm // 8
    inner = lax.rem(tm, 8)
    x = inner // 2
    core = lax.rem(tm, 2)
    slab = slab_x(s, x)
    q = 2 * slab + core

    load_sources = pltpu.make_async_copy(sources_ref.at[0], source_vm, load_sem.at[0])
    load_sources.start()

    barrier = pltpu.get_barrier_semaphore()

    def others(do):
        for away in (2, 1, 3, 0):
            base = 8 * lax.rem(tracer + away, 4)

            def one(j, carry):
                do(base + lax.rem(inner + j, 8))
                return carry

            lax.fori_loop(1 if away == 0 else 0, 8, one, 0)

    def greet(to):
        pl.semaphore_signal(barrier, inc=1, device_id=to, device_id_type=MESH)

    place = 4 * s + slab
    beside = []
    for step in (-1, 1):
        other = lax.rem(place + step + 32, 32)
        other_s = other // 4
        other_x = slab_x(other_s, lax.rem(other, 4))
        beside.append(((tracer * 4 + other_x) * 2 + 1, other_s))

    others(lambda to: greet((to, s)))
    greet(beside[0])

    @pl.when(core == 1)
    def _():
        greet(beside[1])
        greet((beside[1][0] - 1, beside[1][1]))

    load_coarse = pltpu.make_async_copy(
        coarse_ref.at[pl.ds(ROWS * slab + PAIR * core, PAIR)], coarse_vm, load_sem.at[1]
    )
    load_initial = pltpu.make_async_copy(
        initial_ref.at[:, pl.ds(pl.multiple_of(q * PIECE, PIECE), PIECE)], init_vm, load_sem.at[2]
    )
    load_cols = pltpu.make_async_copy(cols_ref, cols_sm, load_sem.at[3])
    load_operator = pltpu.make_async_copy(operator_ref.at[pl.ds(ROWS * slab, ROWS)], op_vm, load_sem.at[4])
    for load in (load_coarse, load_initial, load_cols, load_operator):
        load.start()

    load_sources.wait()
    for piece in range(8):
        for line in range(LINES):
            at = piece * PIECE + line * LANES
            send_vm[4 * piece : 4 * piece + 4, line, :] = source_vm[:, at : at + LANES]
    recv_vm[tm] = send_vm[q * 4 + tracer]

    load_coarse.wait()
    for b in range(PAIR):
        high, low = halves(coarse_vm[b].T)
        high_vm[0, b] = high
        low_vm[0, b] = low

    def square(i):
        level, b = i // PAIR, lax.rem(i, PAIR)
        high, low = high_vm[level, b], low_vm[level, b]
        high, low = halves(dot(high, high) + dot(high, low) + dot(low, high))
        high_vm[level + 1, b] = high
        low_vm[level + 1, b] = low

    pl.semaphore_wait(barrier, 32 + 2 * core)

    def scatter(to):
        to_q = 2 * slab_x(s, lax.rem(to // 2, 4)) + lax.rem(to, 2)
        pltpu.make_async_remote_copy(
            send_vm.at[to_q * 4 + to // 8], recv_vm.at[tm], a2a_sem.at[0], a2a_sem.at[1],
            device_id=(to, s), device_id_type=MESH,
        ).start()

    for first, count in ((0, 2), (2, 6)):
        for away in (2, 1, 3, 0):
            base = 8 * lax.rem(tracer + away, 4) + first

            def one(j, carry):
                to = base + lax.rem(inner + j, count)

                @pl.when(to != tm)
                def _():
                    scatter(to)

                return carry

            lax.fori_loop(0, count, one, 0)

    load_cols.wait()
    load_operator.wait()

    def offset_of(i, j):
        row = ROWS * slab + i
        return lax.rem(cols_sm[j, row] - (16 * s + row) + 256, 128)

    def turn(i):
        offsets = [offset_of(i, j) for j in range(4)]
        for slot in range(4):
            j = 0
            for other in range(1, 4):
                off = offsets[other]
                hit = off == (0, 127, 1)[slot] if slot < 3 else jnp.logical_or(off == 2, off == 126)
                j = jnp.where(hit, other, j)
            opt_vm[i, slot] = op_vm[i, j].T

    def late(i, carry):
        square(i)
        turn(i)
        return carry

    lax.fori_loop(0, ROWS, late, 0)

    def last(b, carry):
        square(ROWS + b)
        return carry

    lax.fori_loop(0, PAIR, last, 0)

    def ahead(i):
        found = [(offset_of(i, j) == 2).astype(jnp.int32) for j in range(4)]
        return (found[0] + found[1] + found[2] + found[3]) > 0

    def all_pieces():
        return pltpu.make_async_remote_copy(
            send_vm.at[pl.ds(0, 31)], recv_vm.at[pl.ds(0, 31)], a2a_sem.at[0], a2a_sem.at[1],
            device_id=(tm, s), device_id_type=MESH,
        )

    load_initial.wait()
    all_pieces().wait_recv()

    def coarse(level, value, b):
        rows = value.shape[0]
        high, low = value.astype(BF16).astype(F32), value
        both = jnp.concatenate([high, low - high], axis=0).astype(BF16)
        got = dot(both, high_vm[level, b]) + dot(both, low_vm[level, b])
        return got[:rows] + got[rows:]

    def scan(values, finish):
        for level in range(LEVELS - 1):
            by = 1 << level
            moved = [coarse(level, value, b) for b, value in enumerate(values)]
            values = [
                value + jnp.concatenate([jnp.zeros((by, BLK), F32), move[: SLICES - by]], axis=0)
                for value, move in zip(values, moved)
            ]
        last = [value[:CHUNK] for value in values]
        finish(0, last)
        for chunk in range(1, SLICES // CHUNK):
            last = [
                value[CHUNK * chunk : CHUNK * (chunk + 1)] + coarse(LEVELS - 1, before, b)
                for b, (value, before) in enumerate(zip(values, last))
            ]
            finish(chunk, last)

    first_row = lax.broadcasted_iota(jnp.int32, (SLICES, BLK), 0) == 0
    forced = []
    for b in range(PAIR):
        source = jnp.concatenate([recv_vm[:, 4 * b + line, :] for line in range(4)], axis=1)
        src_vm[PAIR * core + b] = source * (1.0 / STEPS)
        start = init_vm[pl.ds(tracer, 1), BLK * b : BLK * (b + 1)]
        forced.append(coarse(0, source + jnp.where(first_row, start, 0.0), b))

    def hand(what, ref, to):
        return pltpu.make_async_remote_copy(
            ref.at[pl.ds(0, PAIR)], (v_vm, src_vm, back_vm)[what].at[pl.ds(0, PAIR)], hand_sem.at[what, 0], hand_sem.at[what, 1],
            device_id=(tm - core + to, s), device_id_type=MESH,
        )

    def halo(parity, what, part):
        rows = pl.ds(PART * part, PART)
        return pltpu.make_async_remote_copy(
            w_vm.at[parity, (0, 3, 1, 2)[what], rows], halo_vm.at[parity, what, rows], send_sem.at[parity, what, part],
            recv_sem.at[parity, what, part], device_id=beside[what % 2], device_id_type=MESH,
        )

    @pl.when(core == 0)
    def _():
        hand(1, src_vm, 1).start()

    def keep_end(chunk, last):
        for b in range(PAIR):
            end_vm[b, CHUNK * chunk : CHUNK * (chunk + 1)] = last[b]
        done = CHUNK * (chunk + 1)
        if done % PART:
            return
        part = done // PART - 1
        for b in range(PAIR):
            if part == 0:
                start = init_vm[pl.ds(tracer, 1), BLK * b : BLK * (b + 1)]
                start = jnp.concatenate([start, end_vm[b, : PART - 1]], axis=0)
            else:
                start = end_vm[b, PART * part - 1 : PART * (part + 1) - 1]
            at = slice(PART * part, PART * (part + 1))
            v_vm[PAIR * core + b, at] = start
            w_vm[0, PAIR * core + b, at] = start.astype(BF16)

        @pl.when(core == 0)
        def _():
            halo(0, 0, part).start()
            halo(0, 2, part).start()

        @pl.when(core == 1)
        def _():
            halo(0, 1, part).start()
            halo(0, 3, part).start()

    scan(forced, keep_end)

    @pl.when(core == 0)
    def _():
        hand(0, v_vm, 1).start()
        for part in range(PARTS):
            halo(0, 0, part).wait_send()
            halo(0, 2, part).wait_send()
        hand(0, v_vm, 1).wait_send()
        hand(1, src_vm, 1).wait_send()
        hand(2, v_vm, 1).wait_recv()

    @pl.when(core == 1)
    def _():
        hand(0, v_vm, 0).wait_recv()
        for row in range(PAIR):
            w_vm[0, row] = v_vm[row].astype(BF16)
        hand(1, src_vm, 0).wait_recv()
        signs = [ahead(i) for i in range(ROWS)]

        def fine(i, carry):
            now = lax.rem(i, 2)
            later = 1 - now
            w = [w_vm[now, row] for row in range(ROWS)]
            inside = [
                dot(w[0], opt_vm[0, 0]) + dot(w[1], opt_vm[0, 2]),
                dot(w[0], opt_vm[1, 1]) + dot(w[1], opt_vm[1, 0]) + dot(w[2], opt_vm[1, 2]),
                dot(w[1], opt_vm[2, 1]) + dot(w[2], opt_vm[2, 0]) + dot(w[3], opt_vm[2, 2]),
                dot(w[2], opt_vm[3, 1]) + dot(w[3], opt_vm[3, 0]),
            ]

            @pl.when(i > 0)
            def _():
                for part in range(PARTS):
                    halo(later, 1, part).wait_send()
                    halo(later, 3, part).wait_send()

            @pl.when(i > 1)
            def _():
                for part in range(PARTS):
                    halo(later, 0, part).wait_send()
                    halo(later, 2, part).wait_send()

            for part in range(PARTS):
                at = slice(PART * part, PART * (part + 1))
                for side in range(2):
                    edge, next_in = (0, 1) if side == 0 else (3, 2)
                    toward = 1 + side

                    def update(row, change):
                        value = (v_vm[row, at] + change) + src_vm[row, at]
                        v_vm[row, at] = value
                        w_vm[later, row, at] = value.astype(BF16)

                    def send(what):
                        @pl.when(i < STEPS - 1)
                        def _():
                            halo(later, what, part).start()

                    halo(now, 1 - side, part).wait_recv()
                    near = halo_vm[now, 1 - side, at]
                    change = inside[edge][at] + dot(near, opt_vm[edge, toward])
                    halo(now, 3 - side, part).wait_recv()
                    far = halo_vm[now, 3 - side, at]
                    out = signs[edge] if side == 1 else jnp.logical_not(signs[edge])
                    update(edge, change + dot(jnp.where(out, far, w[3 - next_in][at]), opt_vm[edge, 3]))
                    send(side)
                    out = signs[next_in] if side == 1 else jnp.logical_not(signs[next_in])
                    change = dot(jnp.where(out, near, w[3 - edge][at]), opt_vm[next_in, 3])
                    update(next_in, inside[next_in][at] + change)
                    send(2 + side)

                    if side == 0 and part == PARTS - 1:

                        @pl.when(i == STEPS - 1)
                        def _():
                            hand(2, v_vm, 0).start()

            return carry

        lax.fori_loop(0, STEPS, fine, 0)
        for part in range(PARTS):
            for what in range(4):
                halo((STEPS - 1) % 2, what, part).wait_send()
        hand(2, v_vm, 0).wait_send()

    def send_out(chunk, last):
        for b in range(PAIR):
            ends = end_vm[b, CHUNK * chunk : CHUNK * (chunk + 1)] + last[b]
            for line in range(4):
                osend_vm[CHUNK * chunk : CHUNK * (chunk + 1), 4 * b + line, :] = ends[:, LANES * line : LANES * (line + 1)]

        def one(j, carry):
            to = CHUNK * chunk + lax.rem(inner + j, CHUNK)

            @pl.when(to != tm)
            def _():
                pltpu.make_async_remote_copy(
                    osend_vm.at[to], orecv_vm.at[q * 4 + tracer], a2a_sem.at[2], a2a_sem.at[3],
                    device_id=(to, s), device_id_type=MESH,
                ).start()

            return carry

        lax.fori_loop(0, CHUNK, one, 0)

    scan([jnp.where(core == 0, back_vm[b], v_vm[PAIR + b]) - end_vm[b] for b in range(PAIR)], send_out)
    orecv_vm[q * 4 + tracer] = osend_vm[tm]
    back = pltpu.make_async_remote_copy(
        osend_vm.at[pl.ds(0, 31)], orecv_vm.at[pl.ds(0, 31)], a2a_sem.at[2], a2a_sem.at[3],
        device_id=(tm, s), device_id_type=MESH,
    )
    back.wait_recv()
    for piece in range(8):
        for line in range(LINES):
            at = piece * PIECE + line * LANES
            out_ref[0, :, at : at + LANES] = orecv_vm[4 * piece : 4 * piece + 4, line, :]
    back.wait_send()
    all_pieces().wait_send()


def local(initial, sources, operator, col_blocks, coarse_inv):
    cells = initial.shape[1]
    cols = col_blocks.T
    return pl.pallas_call(
        kernel,
        out_shape=pltpu.VMEM((1, TRACERS, cells), F32),
        in_specs=[
            pl.BlockSpec(memory_space=pltpu.HBM),
            pl.BlockSpec(memory_space=pltpu.HBM),
            pl.BlockSpec(memory_space=pltpu.HBM),
            pl.BlockSpec(memory_space=pltpu.HBM),
            pl.BlockSpec(memory_space=pltpu.HBM),
        ],
        out_specs=pl.BlockSpec(memory_space=pltpu.VMEM),
        scratch_shapes=[
            pltpu.VMEM((TRACERS, cells), F32),
            pltpu.SMEM(cols.shape, jnp.int32),
            pltpu.VMEM((PAIR, BLK, BLK), F32),
            pltpu.VMEM((ROWS, 4, BLK, BLK), BF16),
            pltpu.VMEM((ROWS, 4, BLK, BLK), BF16),
            pltpu.VMEM((LEVELS, PAIR, BLK, BLK), BF16),
            pltpu.VMEM((LEVELS, PAIR, BLK, BLK), BF16),
            pltpu.VMEM((TRACERS, PIECE), F32),
            pltpu.VMEM((SLICES, LINES, LANES), F32),
            pltpu.VMEM((SLICES, LINES, LANES), F32),
            pltpu.VMEM((SLICES, LINES, LANES), F32),
            pltpu.VMEM((SLICES, LINES, LANES), F32),
            pltpu.VMEM((ROWS, SLICES, BLK), F32),
            pltpu.VMEM((ROWS, SLICES, BLK), F32),
            pltpu.VMEM((PAIR, SLICES, BLK), F32),
            pltpu.VMEM((PAIR, SLICES, BLK), F32),
            pltpu.VMEM((2, ROWS, SLICES, BLK), BF16),
            pltpu.VMEM((2, ROWS, SLICES, BLK), BF16),
            pltpu.SemaphoreType.DMA((5,)),
            pltpu.SemaphoreType.DMA((4,)),
            pltpu.SemaphoreType.DMA((3, 2)),
            pltpu.SemaphoreType.DMA((2, 4, PARTS)),
            pltpu.SemaphoreType.DMA((2, 4, PARTS)),
        ],
        compiler_params=pltpu.CompilerParams(
            collective_id=0, has_side_effects=True, vmem_limit_bytes=63 << 20
        ),
        name="parareal",
    )(initial, sources, operator, cols, coarse_inv)


def solution(mesh):
    placed = (
        P(None, "space"),
        P("tm", None, "space"),
        P("space", None, None, None),
        P("space", None),
        P("space", None, None),
    )
    return jax.shard_map(
        local, mesh=mesh, in_specs=placed, out_specs=P("tm", None, "space"), check_vma=False
    )
```

```python
import jax
import jax.numpy as jnp
from jax import lax
from jax.experimental import pallas as pl
from jax.experimental.pallas import tpu as pltpu
from jax.sharding import PartitionSpec as P

MESH = pl.DeviceIdType.MESH
F32 = jnp.float32
BF16 = jnp.bfloat16

TRACERS = 4
BLK = 512
SLICES = 32
STEPS = 8
ROWS = 4
PAIR = 2
PIECE = PAIR * BLK
LANES = 128
LINES = PIECE // LANES
LEVELS = 4
CHUNK = 8
PART = 16
PARTS = SLICES // PART


def slab_x(s, k):
    odd = lax.rem(s, 2)
    return 3 * odd + (1 - 2 * odd) * k


def flipped(s):
    return 1 - lax.rem(s, 4) // 2


def dot(a, b):
    return jnp.dot(a, b, preferred_element_type=F32)


def halves(x):
    high = x.astype(BF16)
    return high, (x - high.astype(F32)).astype(BF16)


def kernel(
    initial_ref, sources_ref, operator_ref, cols_ref, coarse_ref, out_ref,
    source_vm, cols_sm, coarse_vm, op_vm, opt_vm, high_vm, low_vm, init_vm, send_vm, recv_vm, osend_vm, orecv_vm,
    src_vm, v_vm, back_vm, end_vm, w_vm, halo_vm,
    load_sem, a2a_sem, hand_sem, send_sem, recv_sem,
):
    tm = lax.axis_index("tm")
    s = lax.axis_index("space")
    tracer = tm // 8
    inner = lax.rem(tm, 8)
    x = inner // 2
    core = lax.rem(tm, 2)
    slab = slab_x(s, x)
    flip = flipped(s)
    half = core + flip - 2 * core * flip
    q = 2 * slab + half

    def local_row(b):
        return PAIR * core + b + flip * (1 - 2 * b)


    load_sources = pltpu.make_async_copy(sources_ref.at[0], source_vm, load_sem.at[0])
    load_sources.start()

    barrier = pltpu.get_barrier_semaphore()

    def others(do):
        for away in (2, 1, 3, 0):
            base = 8 * lax.rem(tracer + away, 4)

            def one(j, carry):
                do(base + lax.rem(inner + j, 8))
                return carry

            lax.fori_loop(1 if away == 0 else 0, 8, one, 0)

    def greet(to):
        pl.semaphore_signal(barrier, inc=1, device_id=to, device_id_type=MESH)

    place = 4 * s + slab
    beside, their_side = [], []
    for side in range(2):
        other = lax.rem(place + (2 * side - 1) * (1 - 2 * flip) + 32, 32)
        other_s = other // 4
        other_x = slab_x(other_s, lax.rem(other, 4))
        beside.append(((tracer * 4 + other_x) * 2 + 1, other_s))
        turned = flip + flipped(other_s) - 2 * flip * flipped(other_s)
        their_side.append(1 - side + turned * (2 * side - 1))

    others(lambda to: greet((to, s)))
    greet(beside[0])

    @pl.when(core == 1)
    def _():
        greet(beside[1])
        for side in range(2):

            @pl.when(their_side[side] == 0)
            def _():
                greet((beside[side][0] - 1, beside[side][1]))

    load_coarse = pltpu.make_async_copy(
        coarse_ref.at[pl.ds(ROWS * slab + PAIR * half, PAIR)], coarse_vm, load_sem.at[1]
    )
    load_initial = pltpu.make_async_copy(
        initial_ref.at[:, pl.ds(pl.multiple_of(q * PIECE, PIECE), PIECE)], init_vm, load_sem.at[2]
    )
    load_cols = pltpu.make_async_copy(cols_ref, cols_sm, load_sem.at[3])
    load_operator = pltpu.make_async_copy(operator_ref.at[pl.ds(ROWS * slab, ROWS)], op_vm, load_sem.at[4])
    for load in (load_coarse, load_initial, load_cols, load_operator):
        load.start()

    load_sources.wait()
    for piece in range(8):
        for line in range(LINES):
            at = piece * PIECE + line * LANES
            send_vm[4 * piece : 4 * piece + 4, line, :] = source_vm[:, at : at + LANES]
    recv_vm[tm] = send_vm[q * 4 + tracer]

    load_coarse.wait()
    for b in range(PAIR):
        high, low = halves(coarse_vm[b].T)
        high_vm[0, b] = high
        low_vm[0, b] = low

    def square(i):
        level, b = i // PAIR, lax.rem(i, PAIR)
        high, low = high_vm[level, b], low_vm[level, b]
        high, low = halves(dot(high, high) + dot(high, low) + dot(low, high))
        high_vm[level + 1, b] = high
        low_vm[level + 1, b] = low

    pl.semaphore_wait(barrier, 32 + core * (3 - their_side[0] - their_side[1]))

    def scatter(to):
        to_core = lax.rem(to, 2)
        to_q = 2 * slab_x(s, lax.rem(to // 2, 4)) + to_core + flip - 2 * to_core * flip
        pltpu.make_async_remote_copy(
            send_vm.at[to_q * 4 + to // 8], recv_vm.at[tm], a2a_sem.at[0], a2a_sem.at[1],
            device_id=(to, s), device_id_type=MESH,
        ).start()

    for first, count in ((0, 2), (2, 6)):
        for away in (2, 1, 3, 0):
            base = 8 * lax.rem(tracer + away, 4) + first

            def one(j, carry):
                to = base + lax.rem(inner + j, count)

                @pl.when(to != tm)
                def _():
                    scatter(to)

                return carry

            lax.fori_loop(0, count, one, 0)

    load_cols.wait()
    load_operator.wait()

    def offset_of(i, j):
        row = ROWS * slab + i + flip * (ROWS - 1 - 2 * i)
        return lax.rem((cols_sm[j, row] - (16 * s + row)) * (1 - 2 * flip) + 256, 128)

    def turn(i):
        offsets = [offset_of(i, j) for j in range(4)]
        for slot in range(4):
            j = 0
            for other in range(1, 4):
                off = offsets[other]
                hit = off == (0, 127, 1)[slot] if slot < 3 else jnp.logical_or(off == 2, off == 126)
                j = jnp.where(hit, other, j)
            opt_vm[i, slot] = op_vm[i + flip * (ROWS - 1 - 2 * i), j].T

    def late(i, carry):
        square(i)
        turn(i)
        return carry

    lax.fori_loop(0, ROWS, late, 0)

    def last(b, carry):
        square(ROWS + b)
        return carry

    lax.fori_loop(0, PAIR, last, 0)

    def ahead(i):
        found = [(offset_of(i, j) == 2).astype(jnp.int32) for j in range(4)]
        return (found[0] + found[1] + found[2] + found[3]) > 0

    def all_pieces():
        return pltpu.make_async_remote_copy(
            send_vm.at[pl.ds(0, 31)], recv_vm.at[pl.ds(0, 31)], a2a_sem.at[0], a2a_sem.at[1],
            device_id=(tm, s), device_id_type=MESH,
        )

    load_initial.wait()
    all_pieces().wait_recv()

    def coarse(level, value, b):
        rows = value.shape[0]
        high, low = value.astype(BF16).astype(F32), value
        both = jnp.concatenate([high, low - high], axis=0).astype(BF16)
        got = dot(both, high_vm[level, b]) + dot(both, low_vm[level, b])
        return got[:rows] + got[rows:]

    def scan(values, finish):
        for level in range(LEVELS - 1):
            by = 1 << level
            moved = [coarse(level, value, b) for b, value in enumerate(values)]
            values = [
                value + jnp.concatenate([jnp.zeros((by, BLK), F32), move[: SLICES - by]], axis=0)
                for value, move in zip(values, moved)
            ]
        last = [value[:CHUNK] for value in values]
        finish(0, last)
        for chunk in range(1, SLICES // CHUNK):
            last = [
                value[CHUNK * chunk : CHUNK * (chunk + 1)] + coarse(LEVELS - 1, before, b)
                for b, (value, before) in enumerate(zip(values, last))
            ]
            finish(chunk, last)

    first_row = lax.broadcasted_iota(jnp.int32, (SLICES, BLK), 0) == 0
    forced = []
    for b in range(PAIR):
        source = jnp.concatenate([recv_vm[:, 4 * b + line, :] for line in range(4)], axis=1)
        src_vm[local_row(b)] = source * (1.0 / STEPS)
        start = init_vm[pl.ds(tracer, 1), BLK * b : BLK * (b + 1)]
        forced.append(coarse(0, source + jnp.where(first_row, start, 0.0), b))

    def hand(what, ref, to):
        return pltpu.make_async_remote_copy(
            ref.at[pl.ds(0, PAIR)], (v_vm, src_vm, back_vm)[what].at[pl.ds(0, PAIR)], hand_sem.at[what, 0], hand_sem.at[what, 1],
            device_id=(tm - core + to, s), device_id_type=MESH,
        )

    def halo(parity, what, part):
        rows = pl.ds(PART * part, PART)
        slot = what // 2 * 2 + their_side[what % 2]
        return pltpu.make_async_remote_copy(
            w_vm.at[parity, (0, 3, 1, 2)[what], rows], halo_vm.at[parity, slot, rows], send_sem.at[parity, what, part],
            recv_sem.at[parity, slot, part], device_id=beside[what % 2], device_id_type=MESH,
        )

    def halo_in(parity, slot, part):
        rows = pl.ds(PART * part, PART)
        return pltpu.make_async_remote_copy(
            w_vm.at[parity, slot, rows], halo_vm.at[parity, slot, rows], send_sem.at[parity, slot, part],
            recv_sem.at[parity, slot, part], device_id=beside[slot % 2], device_id_type=MESH,
        )

    @pl.when(core == 0)
    def _():
        hand(1, src_vm, 1).start()

    def keep_end(chunk, last):
        for b in range(PAIR):
            end_vm[b, CHUNK * chunk : CHUNK * (chunk + 1)] = last[b]
        done = CHUNK * (chunk + 1)
        if done % PART:
            return
        part = done // PART - 1
        for b in range(PAIR):
            if part == 0:
                start = init_vm[pl.ds(tracer, 1), BLK * b : BLK * (b + 1)]
                start = jnp.concatenate([start, end_vm[b, : PART - 1]], axis=0)
            else:
                start = end_vm[b, PART * part - 1 : PART * (part + 1) - 1]
            at = slice(PART * part, PART * (part + 1))
            v_vm[local_row(b), at] = start
            w_vm[0, local_row(b), at] = start.astype(BF16)

        @pl.when(core == 0)
        def _():
            halo(0, 0, part).start()
            halo(0, 2, part).start()

        @pl.when(core == 1)
        def _():
            halo(0, 1, part).start()
            halo(0, 3, part).start()

    scan(forced, keep_end)

    @pl.when(core == 0)
    def _():
        hand(0, v_vm, 1).start()
        for part in range(PARTS):
            halo(0, 0, part).wait_send()
            halo(0, 2, part).wait_send()
        hand(0, v_vm, 1).wait_send()
        hand(1, src_vm, 1).wait_send()
        hand(2, v_vm, 1).wait_recv()

    @pl.when(core == 1)
    def _():
        hand(0, v_vm, 0).wait_recv()
        for row in range(PAIR):
            w_vm[0, row] = v_vm[row].astype(BF16)
        hand(1, src_vm, 0).wait_recv()
        signs = [ahead(i) for i in range(ROWS)]

        def fine(i, carry):
            now = lax.rem(i, 2)
            later = 1 - now
            w = [w_vm[now, row] for row in range(ROWS)]
            inside = [
                dot(w[0], opt_vm[0, 0]) + dot(w[1], opt_vm[0, 2]),
                dot(w[0], opt_vm[1, 1]) + dot(w[1], opt_vm[1, 0]) + dot(w[2], opt_vm[1, 2]),
                dot(w[1], opt_vm[2, 1]) + dot(w[2], opt_vm[2, 0]) + dot(w[3], opt_vm[2, 2]),
                dot(w[2], opt_vm[3, 1]) + dot(w[3], opt_vm[3, 0]),
            ]

            @pl.when(i > 0)
            def _():
                for part in range(PARTS):
                    halo(later, 1, part).wait_send()
                    halo(later, 3, part).wait_send()

            @pl.when(i > 1)
            def _():
                for part in range(PARTS):
                    halo(later, 0, part).wait_send()
                    halo(later, 2, part).wait_send()

            for part in range(PARTS):
                at = slice(PART * part, PART * (part + 1))
                for side in range(2):
                    edge, next_in = (0, 1) if side == 0 else (3, 2)
                    toward = 1 + side

                    def update(row, change):
                        value = (v_vm[row, at] + change) + src_vm[row, at]
                        v_vm[row, at] = value
                        w_vm[later, row, at] = value.astype(BF16)

                    def send(what):
                        @pl.when(i < STEPS - 1)
                        def _():
                            halo(later, what, part).start()

                    halo_in(now, side, part).wait_recv()
                    near = halo_vm[now, side, at]
                    change = inside[edge][at] + dot(near, opt_vm[edge, toward])
                    halo_in(now, 2 + side, part).wait_recv()
                    far = halo_vm[now, 2 + side, at]
                    out = signs[edge] if side == 1 else jnp.logical_not(signs[edge])
                    update(edge, change + dot(jnp.where(out, far, w[3 - next_in][at]), opt_vm[edge, 3]))
                    send(side)
                    out = signs[next_in] if side == 1 else jnp.logical_not(signs[next_in])
                    change = dot(jnp.where(out, near, w[3 - edge][at]), opt_vm[next_in, 3])
                    update(next_in, inside[next_in][at] + change)
                    send(2 + side)

                    if side == 0 and part == PARTS - 1:

                        @pl.when(i == STEPS - 1)
                        def _():
                            hand(2, v_vm, 0).start()

            return carry

        lax.fori_loop(0, STEPS, fine, 0)
        for part in range(PARTS):
            for what in range(4):
                halo((STEPS - 1) % 2, what, part).wait_send()
        hand(2, v_vm, 0).wait_send()

    def send_out(chunk, last):
        for b in range(PAIR):
            ends = end_vm[b, CHUNK * chunk : CHUNK * (chunk + 1)] + last[b]
            for line in range(4):
                osend_vm[CHUNK * chunk : CHUNK * (chunk + 1), 4 * b + line, :] = ends[:, LANES * line : LANES * (line + 1)]

        def one(j, carry):
            to = CHUNK * chunk + lax.rem(inner + j, CHUNK)

            @pl.when(to != tm)
            def _():
                pltpu.make_async_remote_copy(
                    osend_vm.at[to], orecv_vm.at[q * 4 + tracer], a2a_sem.at[2], a2a_sem.at[3],
                    device_id=(to, s), device_id_type=MESH,
                ).start()

            return carry

        lax.fori_loop(0, CHUNK, one, 0)

    def result(b):
        at = b + flip * (1 - 2 * b)
        return jnp.where(core == 0, back_vm[at], v_vm[PAIR + at])

    scan([result(b) - end_vm[b] for b in range(PAIR)], send_out)
    orecv_vm[q * 4 + tracer] = osend_vm[tm]
    back = pltpu.make_async_remote_copy(
        osend_vm.at[pl.ds(0, 31)], orecv_vm.at[pl.ds(0, 31)], a2a_sem.at[2], a2a_sem.at[3],
        device_id=(tm, s), device_id_type=MESH,
    )
    back.wait_recv()
    for piece in range(8):
        for line in range(LINES):
            at = piece * PIECE + line * LANES
            out_ref[0, :, at : at + LANES] = orecv_vm[4 * piece : 4 * piece + 4, line, :]
    back.wait_send()
    all_pieces().wait_send()


def local(initial, sources, operator, col_blocks, coarse_inv):
    cells = initial.shape[1]
    cols = col_blocks.T
    return pl.pallas_call(
        kernel,
        out_shape=pltpu.VMEM((1, TRACERS, cells), F32),
        in_specs=[
            pl.BlockSpec(memory_space=pltpu.HBM),
            pl.BlockSpec(memory_space=pltpu.HBM),
            pl.BlockSpec(memory_space=pltpu.HBM),
            pl.BlockSpec(memory_space=pltpu.HBM),
            pl.BlockSpec(memory_space=pltpu.HBM),
        ],
        out_specs=pl.BlockSpec(memory_space=pltpu.VMEM),
        scratch_shapes=[
            pltpu.VMEM((TRACERS, cells), F32),
            pltpu.SMEM(cols.shape, jnp.int32),
            pltpu.VMEM((PAIR, BLK, BLK), F32),
            pltpu.VMEM((ROWS, 4, BLK, BLK), BF16),
            pltpu.VMEM((ROWS, 4, BLK, BLK), BF16),
            pltpu.VMEM((LEVELS, PAIR, BLK, BLK), BF16),
            pltpu.VMEM((LEVELS, PAIR, BLK, BLK), BF16),
            pltpu.VMEM((TRACERS, PIECE), F32),
            pltpu.VMEM((SLICES, LINES, LANES), F32),
            pltpu.VMEM((SLICES, LINES, LANES), F32),
            pltpu.VMEM((SLICES, LINES, LANES), F32),
            pltpu.VMEM((SLICES, LINES, LANES), F32),
            pltpu.VMEM((ROWS, SLICES, BLK), F32),
            pltpu.VMEM((ROWS, SLICES, BLK), F32),
            pltpu.VMEM((PAIR, SLICES, BLK), F32),
            pltpu.VMEM((PAIR, SLICES, BLK), F32),
            pltpu.VMEM((2, ROWS, SLICES, BLK), BF16),
            pltpu.VMEM((2, ROWS, SLICES, BLK), BF16),
            pltpu.SemaphoreType.DMA((5,)),
            pltpu.SemaphoreType.DMA((4,)),
            pltpu.SemaphoreType.DMA((3, 2)),
            pltpu.SemaphoreType.DMA((2, 4, PARTS)),
            pltpu.SemaphoreType.DMA((2, 4, PARTS)),
        ],
        compiler_params=pltpu.CompilerParams(
            collective_id=0, has_side_effects=True, vmem_limit_bytes=63 << 20
        ),
        name="parareal",
    )(initial, sources, operator, cols, coarse_inv)


def solution(mesh):
    placed = (
        P(None, "space"),
        P("tm", None, "space"),
        P("space", None, None, None),
        P("space", None),
        P("space", None, None),
    )
    return jax.shard_map(
        local, mesh=mesh, in_specs=placed, out_specs=P("tm", None, "space"), check_vma=False
    )
```

```python
import jax
import jax.numpy as jnp
from jax import lax
from jax.experimental import pallas as pl
from jax.experimental.pallas import tpu as pltpu
from jax.sharding import PartitionSpec as P

MESH = pl.DeviceIdType.MESH
F32 = jnp.float32
BF16 = jnp.bfloat16

TRACERS = 4
BLK = 512
SLICES = 32
STEPS = 8
ROWS = 4
PAIR = 2
PIECE = PAIR * BLK
LANES = 128
LINES = PIECE // LANES
LEVELS = 4
CHUNK = 8
PART = 16
PARTS = SLICES // PART
SPAN = 256
SPANS = BLK // SPAN


def slab_x(s, k):
    odd = lax.rem(s, 2)
    return 3 * odd + (1 - 2 * odd) * k


def flipped(s):
    return 1 - lax.rem(s, 4) // 2


def dot(a, b):
    return jnp.dot(a, b, preferred_element_type=F32)


def halves(x):
    high = x.astype(BF16)
    return high, (x - high.astype(F32)).astype(BF16)


def kernel(
    initial_ref, sources_ref, operator_ref, cols_ref, coarse_ref, out_ref,
    source_vm, cols_sm, coarse_vm, op_vm, opt_vm, high_vm, low_vm, init_vm, send_vm, recv_vm, osend_vm, orecv_vm,
    src_vm, v_vm, back_vm, end_vm, w_vm, halo_vm,
    load_sem, a2a_sem, hand_sem, send_sem, recv_sem,
):
    tm = lax.axis_index("tm")
    s = lax.axis_index("space")
    tracer = tm // 8
    inner = lax.rem(tm, 8)
    x = inner // 2
    core = lax.rem(tm, 2)
    slab = slab_x(s, x)
    flip = flipped(s)
    half = core + flip - 2 * core * flip
    q = 2 * slab + half

    def local_row(b):
        return PAIR * core + b + flip * (1 - 2 * b)


    load_sources = pltpu.make_async_copy(sources_ref.at[0], source_vm, load_sem.at[0])
    load_sources.start()

    barrier = pltpu.get_barrier_semaphore()

    def others(do):
        for away in (2, 1, 3, 0):
            base = 8 * lax.rem(tracer + away, 4)

            def one(j, carry):
                do(base + lax.rem(inner + j, 8))
                return carry

            lax.fori_loop(1 if away == 0 else 0, 8, one, 0)

    def greet(to):
        pl.semaphore_signal(barrier, inc=1, device_id=to, device_id_type=MESH)

    place = 4 * s + slab
    beside, their_side = [], []
    for side in range(2):
        other = lax.rem(place + (2 * side - 1) * (1 - 2 * flip) + 32, 32)
        other_s = other // 4
        other_x = slab_x(other_s, lax.rem(other, 4))
        beside.append(((tracer * 4 + other_x) * 2 + 1, other_s))
        turned = flip + flipped(other_s) - 2 * flip * flipped(other_s)
        their_side.append(1 - side + turned * (2 * side - 1))

    others(lambda to: greet((to, s)))
    greet(beside[0])

    @pl.when(core == 1)
    def _():
        greet(beside[1])
        for side in range(2):

            @pl.when(their_side[side] == 0)
            def _():
                greet((beside[side][0] - 1, beside[side][1]))

    load_coarse = pltpu.make_async_copy(
        coarse_ref.at[pl.ds(ROWS * slab + PAIR * half, PAIR)], coarse_vm, load_sem.at[1]
    )
    load_initial = pltpu.make_async_copy(
        initial_ref.at[:, pl.ds(pl.multiple_of(q * PIECE, PIECE), PIECE)], init_vm, load_sem.at[2]
    )
    load_cols = pltpu.make_async_copy(cols_ref, cols_sm, load_sem.at[3])
    load_operator = pltpu.make_async_copy(operator_ref.at[pl.ds(ROWS * slab, ROWS)], op_vm, load_sem.at[4])
    for load in (load_coarse, load_initial, load_cols, load_operator):
        load.start()

    load_sources.wait()
    for piece in range(8):
        for line in range(LINES):
            at = piece * PIECE + line * LANES
            send_vm[4 * piece : 4 * piece + 4, line, :] = source_vm[:, at : at + LANES]
    recv_vm[tm] = send_vm[q * 4 + tracer]

    load_coarse.wait()
    for b in range(PAIR):
        high, low = halves(coarse_vm[b].T)
        high_vm[0, b] = high
        low_vm[0, b] = low

    def square(i):
        level, b = i // PAIR, lax.rem(i, PAIR)
        high, low = high_vm[level, b], low_vm[level, b]
        high, low = halves(dot(high, high) + dot(high, low) + dot(low, high))
        high_vm[level + 1, b] = high
        low_vm[level + 1, b] = low

    pl.semaphore_wait(barrier, 32 + core * (3 - their_side[0] - their_side[1]))

    def scatter(to):
        to_core = lax.rem(to, 2)
        to_q = 2 * slab_x(s, lax.rem(to // 2, 4)) + to_core + flip - 2 * to_core * flip
        pltpu.make_async_remote_copy(
            send_vm.at[to_q * 4 + to // 8], recv_vm.at[tm], a2a_sem.at[0], a2a_sem.at[1],
            device_id=(to, s), device_id_type=MESH,
        ).start()

    for first, count in ((0, 2), (2, 6)):
        for away in (2, 1, 3, 0):
            base = 8 * lax.rem(tracer + away, 4) + first

            def one(j, carry):
                to = base + lax.rem(inner + j, count)

                @pl.when(to != tm)
                def _():
                    scatter(to)

                return carry

            lax.fori_loop(0, count, one, 0)

    load_cols.wait()
    load_operator.wait()

    def offset_of(i, j):
        row = ROWS * slab + i + flip * (ROWS - 1 - 2 * i)
        return lax.rem((cols_sm[j, row] - (16 * s + row)) * (1 - 2 * flip) + 256, 128)

    def turn(i):
        offsets = [offset_of(i, j) for j in range(4)]
        for slot in range(4):
            j = 0
            for other in range(1, 4):
                off = offsets[other]
                hit = off == (0, 127, 1)[slot] if slot < 3 else jnp.logical_or(off == 2, off == 126)
                j = jnp.where(hit, other, j)
            opt_vm[i, slot] = op_vm[i + flip * (ROWS - 1 - 2 * i), j].T

    def late(i, carry):
        square(i)
        turn(i)
        return carry

    lax.fori_loop(0, ROWS, late, 0)

    def last(b, carry):
        square(ROWS + b)
        return carry

    lax.fori_loop(0, PAIR, last, 0)

    def ahead(i):
        found = [(offset_of(i, j) == 2).astype(jnp.int32) for j in range(4)]
        return (found[0] + found[1] + found[2] + found[3]) > 0

    def all_pieces():
        return pltpu.make_async_remote_copy(
            send_vm.at[pl.ds(0, 31)], recv_vm.at[pl.ds(0, 31)], a2a_sem.at[0], a2a_sem.at[1],
            device_id=(tm, s), device_id_type=MESH,
        )

    load_initial.wait()
    all_pieces().wait_recv()

    def coarse(level, value, b):
        rows = value.shape[0]
        high, low = value.astype(BF16).astype(F32), value
        both = jnp.concatenate([high, low - high], axis=0).astype(BF16)
        got = dot(both, high_vm[level, b]) + dot(both, low_vm[level, b])
        return got[:rows] + got[rows:]

    def scan(values, finish):
        for level in range(LEVELS - 1):
            by = 1 << level
            moved = [coarse(level, value, b) for b, value in enumerate(values)]
            values = [
                value + jnp.concatenate([jnp.zeros((by, BLK), F32), move[: SLICES - by]], axis=0)
                for value, move in zip(values, moved)
            ]
        last = [value[:CHUNK] for value in values]
        finish(0, last)
        for chunk in range(1, SLICES // CHUNK):
            last = [
                value[CHUNK * chunk : CHUNK * (chunk + 1)] + coarse(LEVELS - 1, before, b)
                for b, (value, before) in enumerate(zip(values, last))
            ]
            finish(chunk, last)

    first_row = lax.broadcasted_iota(jnp.int32, (SLICES, BLK), 0) == 0
    forced = []
    for b in range(PAIR):
        source = jnp.concatenate([recv_vm[:, 4 * b + line, :] for line in range(4)], axis=1)
        src_vm[local_row(b)] = source * (1.0 / STEPS)
        start = init_vm[pl.ds(tracer, 1), BLK * b : BLK * (b + 1)]
        forced.append(coarse(0, source + jnp.where(first_row, start, 0.0), b))

    def hand(what, ref, to):
        return pltpu.make_async_remote_copy(
            ref.at[pl.ds(0, PAIR)], (v_vm, src_vm, back_vm)[what].at[pl.ds(0, PAIR)], hand_sem.at[what, 0], hand_sem.at[what, 1],
            device_id=(tm - core + to, s), device_id_type=MESH,
        )

    def halo(parity, what, part, span):
        rows, columns = pl.ds(PART * part, PART), pl.ds(SPAN * span, SPAN)
        slot = what // 2 * 2 + their_side[what % 2]
        return pltpu.make_async_remote_copy(
            w_vm.at[parity, (0, 3, 1, 2)[what], rows, columns], halo_vm.at[parity, slot, rows, columns], send_sem.at[parity, what, part, span],
            recv_sem.at[parity, slot, part, span], device_id=beside[what % 2], device_id_type=MESH,
        )

    def halo_in(parity, slot, part, span):
        rows, columns = pl.ds(PART * part, PART), pl.ds(SPAN * span, SPAN)
        return pltpu.make_async_remote_copy(
            w_vm.at[parity, slot, rows, columns], halo_vm.at[parity, slot, rows, columns], send_sem.at[parity, slot, part, span],
            recv_sem.at[parity, slot, part, span], device_id=beside[slot % 2], device_id_type=MESH,
        )

    @pl.when(core == 0)
    def _():
        hand(1, src_vm, 1).start()

    def keep_end(chunk, last):
        for b in range(PAIR):
            end_vm[b, CHUNK * chunk : CHUNK * (chunk + 1)] = last[b]
        done = CHUNK * (chunk + 1)
        if done % PART:
            return
        part = done // PART - 1
        for b in range(PAIR):
            if part == 0:
                start = init_vm[pl.ds(tracer, 1), BLK * b : BLK * (b + 1)]
                start = jnp.concatenate([start, end_vm[b, : PART - 1]], axis=0)
            else:
                start = end_vm[b, PART * part - 1 : PART * (part + 1) - 1]
            at = slice(PART * part, PART * (part + 1))
            v_vm[local_row(b), at] = start
            w_vm[0, local_row(b), at] = start.astype(BF16)

        @pl.when(core == 0)
        def _():
            for span in range(SPANS):
                halo(0, 0, part, span).start()
            for span in range(SPANS):
                halo(0, 2, part, span).start()

        @pl.when(core == 1)
        def _():
            for span in range(SPANS):
                halo(0, 1, part, span).start()
            for span in range(SPANS):
                halo(0, 3, part, span).start()

    scan(forced, keep_end)

    @pl.when(core == 0)
    def _():
        hand(0, v_vm, 1).start()
        for part in range(PARTS):
            for span in range(SPANS):
                halo(0, 0, part, span).wait_send()
            for span in range(SPANS):
                halo(0, 2, part, span).wait_send()
        hand(0, v_vm, 1).wait_send()
        hand(1, src_vm, 1).wait_send()
        hand(2, v_vm, 1).wait_recv()

    @pl.when(core == 1)
    def _():
        hand(0, v_vm, 0).wait_recv()
        for row in range(PAIR):
            w_vm[0, row] = v_vm[row].astype(BF16)
        hand(1, src_vm, 0).wait_recv()
        signs = [ahead(i) for i in range(ROWS)]

        def fine(i, carry):
            now = lax.rem(i, 2)
            later = 1 - now
            w = [w_vm[now, row] for row in range(ROWS)]
            inside = [
                dot(w[0], opt_vm[0, 0]) + dot(w[1], opt_vm[0, 2]),
                dot(w[0], opt_vm[1, 1]) + dot(w[1], opt_vm[1, 0]) + dot(w[2], opt_vm[1, 2]),
                dot(w[1], opt_vm[2, 1]) + dot(w[2], opt_vm[2, 0]) + dot(w[3], opt_vm[2, 2]),
                dot(w[2], opt_vm[3, 1]) + dot(w[3], opt_vm[3, 0]),
            ]

            @pl.when(i > 0)
            def _():
                for part in range(PARTS):
                    for span in range(SPANS):
                        halo(later, 1, part, span).wait_send()
                    for span in range(SPANS):
                        halo(later, 3, part, span).wait_send()

            @pl.when(i > 1)
            def _():
                for part in range(PARTS):
                    for span in range(SPANS):
                        halo(later, 0, part, span).wait_send()
                    for span in range(SPANS):
                        halo(later, 2, part, span).wait_send()

            for part in range(PARTS):
                at = slice(PART * part, PART * (part + 1))
                for side in range(2):
                    edge, next_in = (0, 1) if side == 0 else (3, 2)
                    toward = 1 + side

                    def update(row, change, value, what):
                        for span in range(SPANS):
                            columns = slice(SPAN * span, SPAN * (span + 1))
                            total = change[:, columns] + dot(value, opt_vm[row, 3, :, columns])
                            total = (v_vm[row, at, columns] + total) + src_vm[row, at, columns]
                            v_vm[row, at, columns] = total
                            w_vm[later, row, at, columns] = total.astype(BF16)

                            @pl.when(i < STEPS - 1)
                            def _():
                                halo(later, what, part, span).start()

                    for span in range(SPANS):
                        halo_in(now, side, part, span).wait_recv()
                    near = halo_vm[now, side, at]
                    change = inside[edge][at] + dot(near, opt_vm[edge, toward])
                    for span in range(SPANS):
                        halo_in(now, 2 + side, part, span).wait_recv()
                    far = halo_vm[now, 2 + side, at]
                    out = signs[edge] if side == 1 else jnp.logical_not(signs[edge])
                    update(edge, change, jnp.where(out, far, w[3 - next_in][at]), side)
                    out = signs[next_in] if side == 1 else jnp.logical_not(signs[next_in])
                    update(next_in, inside[next_in][at], jnp.where(out, near, w[3 - edge][at]), 2 + side)

                    if side == 0 and part == PARTS - 1:

                        @pl.when(i == STEPS - 1)
                        def _():
                            hand(2, v_vm, 0).start()

            return carry

        lax.fori_loop(0, STEPS, fine, 0)
        for part in range(PARTS):
            for what in range(4):
                for span in range(SPANS):
                    halo((STEPS - 1) % 2, what, part, span).wait_send()
        hand(2, v_vm, 0).wait_send()

    def send_out(chunk, last):
        for b in range(PAIR):
            ends = end_vm[b, CHUNK * chunk : CHUNK * (chunk + 1)] + last[b]
            for line in range(4):
                osend_vm[CHUNK * chunk : CHUNK * (chunk + 1), 4 * b + line, :] = ends[:, LANES * line : LANES * (line + 1)]

        def one(j, carry):
            to = CHUNK * chunk + lax.rem(inner + j, CHUNK)

            @pl.when(to != tm)
            def _():
                pltpu.make_async_remote_copy(
                    osend_vm.at[to], orecv_vm.at[q * 4 + tracer], a2a_sem.at[2], a2a_sem.at[3],
                    device_id=(to, s), device_id_type=MESH,
                ).start()

            return carry

        lax.fori_loop(0, CHUNK, one, 0)

    def result(b):
        at = b + flip * (1 - 2 * b)
        return jnp.where(core == 0, back_vm[at], v_vm[PAIR + at])

    scan([result(b) - end_vm[b] for b in range(PAIR)], send_out)
    orecv_vm[q * 4 + tracer] = osend_vm[tm]
    back = pltpu.make_async_remote_copy(
        osend_vm.at[pl.ds(0, 31)], orecv_vm.at[pl.ds(0, 31)], a2a_sem.at[2], a2a_sem.at[3],
        device_id=(tm, s), device_id_type=MESH,
    )
    back.wait_recv()
    for piece in range(8):
        for line in range(LINES):
            at = piece * PIECE + line * LANES
            out_ref[0, :, at : at + LANES] = orecv_vm[4 * piece : 4 * piece + 4, line, :]
    back.wait_send()
    all_pieces().wait_send()


def local(initial, sources, operator, col_blocks, coarse_inv):
    cells = initial.shape[1]
    cols = col_blocks.T
    return pl.pallas_call(
        kernel,
        out_shape=pltpu.VMEM((1, TRACERS, cells), F32),
        in_specs=[
            pl.BlockSpec(memory_space=pltpu.HBM),
            pl.BlockSpec(memory_space=pltpu.HBM),
            pl.BlockSpec(memory_space=pltpu.HBM),
            pl.BlockSpec(memory_space=pltpu.HBM),
            pl.BlockSpec(memory_space=pltpu.HBM),
        ],
        out_specs=pl.BlockSpec(memory_space=pltpu.VMEM),
        scratch_shapes=[
            pltpu.VMEM((TRACERS, cells), F32),
            pltpu.SMEM(cols.shape, jnp.int32),
            pltpu.VMEM((PAIR, BLK, BLK), F32),
            pltpu.VMEM((ROWS, 4, BLK, BLK), BF16),
            pltpu.VMEM((ROWS, 4, BLK, BLK), BF16),
            pltpu.VMEM((LEVELS, PAIR, BLK, BLK), BF16),
            pltpu.VMEM((LEVELS, PAIR, BLK, BLK), BF16),
            pltpu.VMEM((TRACERS, PIECE), F32),
            pltpu.VMEM((SLICES, LINES, LANES), F32),
            pltpu.VMEM((SLICES, LINES, LANES), F32),
            pltpu.VMEM((SLICES, LINES, LANES), F32),
            pltpu.VMEM((SLICES, LINES, LANES), F32),
            pltpu.VMEM((ROWS, SLICES, BLK), F32),
            pltpu.VMEM((ROWS, SLICES, BLK), F32),
            pltpu.VMEM((PAIR, SLICES, BLK), F32),
            pltpu.VMEM((PAIR, SLICES, BLK), F32),
            pltpu.VMEM((2, ROWS, SLICES, BLK), BF16),
            pltpu.VMEM((2, ROWS, SLICES, BLK), BF16),
            pltpu.SemaphoreType.DMA((5,)),
            pltpu.SemaphoreType.DMA((4,)),
            pltpu.SemaphoreType.DMA((3, 2)),
            pltpu.SemaphoreType.DMA((2, 4, PARTS, SPANS)),
            pltpu.SemaphoreType.DMA((2, 4, PARTS, SPANS)),
        ],
        compiler_params=pltpu.CompilerParams(
            collective_id=0, has_side_effects=True, vmem_limit_bytes=63 << 20
        ),
        name="parareal",
    )(initial, sources, operator, cols, coarse_inv)


def solution(mesh):
    placed = (
        P(None, "space"),
        P("tm", None, "space"),
        P("space", None, None, None),
        P("space", None),
        P("space", None, None),
    )
    return jax.shard_map(
        local, mesh=mesh, in_specs=placed, out_specs=P("tm", None, "space"), check_vma=False
    )
```

```python
import jax
import jax.numpy as jnp
from jax import lax
from jax.experimental import pallas as pl
from jax.experimental.pallas import tpu as pltpu
from jax.sharding import PartitionSpec as P

MESH = pl.DeviceIdType.MESH
F32 = jnp.float32
BF16 = jnp.bfloat16

TRACERS = 4
BLK = 512
SLICES = 32
STEPS = 8
ROWS = 4
PAIR = 2
PIECE = PAIR * BLK
LANES = 128
LINES = PIECE // LANES
LEVELS = 4
CHUNK = 8
PART = 16
PARTS = SLICES // PART


def slab_x(s, k):
    odd = lax.rem(s, 2)
    return 3 * odd + (1 - 2 * odd) * k


def flipped(s):
    return 1 - lax.rem(s, 4) // 2


def dot(a, b):
    return jnp.dot(a, b, preferred_element_type=F32)


def halves(x):
    high = x.astype(BF16)
    return high, (x - high.astype(F32)).astype(BF16)


def kernel(
    initial_ref, sources_ref, operator_ref, cols_ref, coarse_ref, out_ref,
    source_vm, cols_sm, coarse_vm, op_vm, opt_vm, high_vm, low_vm, init_vm, send_vm, recv_vm, osend_vm, orecv_vm,
    src_vm, v_vm, back_vm, end_vm, w_vm, halo_vm,
    load_sem, a2a_sem, hand_sem, send_sem, recv_sem,
):
    tm = lax.axis_index("tm")
    s = lax.axis_index("space")
    tracer = tm // 8
    inner = lax.rem(tm, 8)
    x = inner // 2
    core = lax.rem(tm, 2)
    slab = slab_x(s, x)
    flip = flipped(s)
    half = core + flip - 2 * core * flip
    q = 2 * slab + half

    def local_row(b):
        return PAIR * core + b + flip * (1 - 2 * b)


    load_sources = pltpu.make_async_copy(sources_ref.at[0], source_vm, load_sem.at[0])
    load_sources.start()

    barrier = pltpu.get_barrier_semaphore()

    def others(do):
        for away in (2, 1, 3, 0):
            base = 8 * lax.rem(tracer + away, 4)

            def one(j, carry):
                do(base + lax.rem(inner + j, 8))
                return carry

            lax.fori_loop(1 if away == 0 else 0, 8, one, 0)

    def greet(to):
        pl.semaphore_signal(barrier, inc=1, device_id=to, device_id_type=MESH)

    place = 4 * s + slab
    beside, their_side = [], []
    for side in range(2):
        other = lax.rem(place + (2 * side - 1) * (1 - 2 * flip) + 32, 32)
        other_s = other // 4
        other_x = slab_x(other_s, lax.rem(other, 4))
        beside.append(((tracer * 4 + other_x) * 2 + 1, other_s))
        turned = flip + flipped(other_s) - 2 * flip * flipped(other_s)
        their_side.append(1 - side + turned * (2 * side - 1))

    others(lambda to: greet((to, s)))
    greet(beside[0])

    @pl.when(core == 1)
    def _():
        greet(beside[1])
        for side in range(2):

            @pl.when(their_side[side] == 0)
            def _():
                greet((beside[side][0] - 1, beside[side][1]))

    load_coarse = pltpu.make_async_copy(
        coarse_ref.at[pl.ds(ROWS * slab + PAIR * half, PAIR)], coarse_vm, load_sem.at[1]
    )
    load_initial = pltpu.make_async_copy(
        initial_ref.at[:, pl.ds(pl.multiple_of(q * PIECE, PIECE), PIECE)], init_vm, load_sem.at[2]
    )
    load_cols = pltpu.make_async_copy(cols_ref, cols_sm, load_sem.at[3])
    load_operator = pltpu.make_async_copy(operator_ref.at[pl.ds(ROWS * slab, ROWS)], op_vm, load_sem.at[4])
    for load in (load_coarse, load_initial, load_cols, load_operator):
        load.start()

    load_sources.wait()
    for piece in range(8):
        for line in range(LINES):
            at = piece * PIECE + line * LANES
            send_vm[4 * piece : 4 * piece + 4, line, :] = source_vm[:, at : at + LANES]
    recv_vm[tm] = send_vm[q * 4 + tracer]

    load_coarse.wait()
    for b in range(PAIR):
        high, low = halves(coarse_vm[b].T)
        high_vm[0, b] = high
        low_vm[0, b] = low

    def square(i):
        level, b = i // PAIR, lax.rem(i, PAIR)
        high, low = high_vm[level, b], low_vm[level, b]
        high, low = halves(dot(high, high) + dot(high, low) + dot(low, high))
        high_vm[level + 1, b] = high
        low_vm[level + 1, b] = low

    pl.semaphore_wait(barrier, 32 + core * (3 - their_side[0] - their_side[1]))

    def scatter(to):
        to_core = lax.rem(to, 2)
        to_q = 2 * slab_x(s, lax.rem(to // 2, 4)) + to_core + flip - 2 * to_core * flip
        pltpu.make_async_remote_copy(
            send_vm.at[to_q * 4 + to // 8], recv_vm.at[tm], a2a_sem.at[0], a2a_sem.at[1],
            device_id=(to, s), device_id_type=MESH,
        ).start()

    for first, count in ((0, 2), (2, 6)):
        for away in (2, 1, 3, 0):
            base = 8 * lax.rem(tracer + away, 4) + first

            def one(j, carry):
                to = base + lax.rem(inner + j, count)

                @pl.when(to != tm)
                def _():
                    scatter(to)

                return carry

            lax.fori_loop(0, count, one, 0)

    load_cols.wait()
    load_operator.wait()

    def offset_of(i, j):
        row = ROWS * slab + i + flip * (ROWS - 1 - 2 * i)
        return lax.rem((cols_sm[j, row] - (16 * s + row)) * (1 - 2 * flip) + 256, 128)

    def turn(i):
        offsets = [offset_of(i, j) for j in range(4)]
        for slot in range(4):
            j = 0
            for other in range(1, 4):
                off = offsets[other]
                hit = off == (0, 127, 1)[slot] if slot < 3 else jnp.logical_or(off == 2, off == 126)
                j = jnp.where(hit, other, j)
            opt_vm[i, slot] = op_vm[i + flip * (ROWS - 1 - 2 * i), j].T

    def late(i, carry):
        square(i)
        turn(i)
        return carry

    lax.fori_loop(0, ROWS, late, 0)

    def last(b, carry):
        square(ROWS + b)
        return carry

    lax.fori_loop(0, PAIR, last, 0)

    def ahead(i):
        found = [(offset_of(i, j) == 2).astype(jnp.int32) for j in range(4)]
        return (found[0] + found[1] + found[2] + found[3]) > 0

    def all_pieces():
        return pltpu.make_async_remote_copy(
            send_vm.at[pl.ds(0, 31)], recv_vm.at[pl.ds(0, 31)], a2a_sem.at[0], a2a_sem.at[1],
            device_id=(tm, s), device_id_type=MESH,
        )

    load_initial.wait()
    all_pieces().wait_recv()

    def coarse(level, value, b):
        rows = value.shape[0]
        high, low = value.astype(BF16).astype(F32), value
        both = jnp.concatenate([high, low - high], axis=0).astype(BF16)
        got = dot(both, high_vm[level, b]) + dot(both, low_vm[level, b])
        return got[:rows] + got[rows:]

    def scan(values, finish):
        for level in range(LEVELS - 1):
            by = 1 << level
            moved = [coarse(level, value, b) for b, value in enumerate(values)]
            values = [
                value + jnp.concatenate([jnp.zeros((by, BLK), F32), move[: SLICES - by]], axis=0)
                for value, move in zip(values, moved)
            ]
        last = [value[:CHUNK] for value in values]
        finish(0, last)
        for chunk in range(1, SLICES // CHUNK):
            last = [
                value[CHUNK * chunk : CHUNK * (chunk + 1)] + coarse(LEVELS - 1, before, b)
                for b, (value, before) in enumerate(zip(values, last))
            ]
            finish(chunk, last)

    first_row = lax.broadcasted_iota(jnp.int32, (SLICES, BLK), 0) == 0
    forced = []
    for b in range(PAIR):
        source = jnp.concatenate([recv_vm[:, 4 * b + line, :] for line in range(4)], axis=1)
        src_vm[local_row(b)] = source * (1.0 / STEPS)
        start = init_vm[pl.ds(tracer, 1), BLK * b : BLK * (b + 1)]
        forced.append(coarse(0, source + jnp.where(first_row, start, 0.0), b))

    def hand(what, ref, to):
        return pltpu.make_async_remote_copy(
            ref.at[pl.ds(0, PAIR)], (v_vm, src_vm, back_vm)[what].at[pl.ds(0, PAIR)], hand_sem.at[what, 0], hand_sem.at[what, 1],
            device_id=(tm - core + to, s), device_id_type=MESH,
        )

    def halo(parity, side, part):
        rows = pl.ds(PART * part, PART)
        slot = their_side[side]
        return pltpu.make_async_remote_copy(
            w_vm.at[parity, pl.ds(PAIR * side, PAIR), rows], halo_vm.at[parity, slot, pl.ds(0, PAIR), rows],
            send_sem.at[parity, side, part], recv_sem.at[parity, slot, part], device_id=beside[side], device_id_type=MESH,
        )

    def halo_in(parity, slot, part):
        rows = pl.ds(PART * part, PART)
        return pltpu.make_async_remote_copy(
            w_vm.at[parity, pl.ds(PAIR * slot, PAIR), rows], halo_vm.at[parity, slot, pl.ds(0, PAIR), rows],
            send_sem.at[parity, slot, part], recv_sem.at[parity, slot, part], device_id=beside[slot], device_id_type=MESH,
        )

    @pl.when(core == 0)
    def _():
        hand(1, src_vm, 1).start()

    def keep_end(chunk, last):
        for b in range(PAIR):
            end_vm[b, CHUNK * chunk : CHUNK * (chunk + 1)] = last[b]
        done = CHUNK * (chunk + 1)
        if done % PART:
            return
        part = done // PART - 1
        for b in range(PAIR):
            if part == 0:
                start = init_vm[pl.ds(tracer, 1), BLK * b : BLK * (b + 1)]
                start = jnp.concatenate([start, end_vm[b, : PART - 1]], axis=0)
            else:
                start = end_vm[b, PART * part - 1 : PART * (part + 1) - 1]
            at = slice(PART * part, PART * (part + 1))
            v_vm[local_row(b), at] = start
            w_vm[0, local_row(b), at] = start.astype(BF16)

        @pl.when(core == 0)
        def _():
            halo(0, 0, part).start()

        @pl.when(core == 1)
        def _():
            halo(0, 1, part).start()

    scan(forced, keep_end)

    @pl.when(core == 0)
    def _():
        hand(0, v_vm, 1).start()
        for part in range(PARTS):
            halo(0, 0, part).wait_send()
        hand(0, v_vm, 1).wait_send()
        hand(1, src_vm, 1).wait_send()
        hand(2, v_vm, 1).wait_recv()

    @pl.when(core == 1)
    def _():
        hand(0, v_vm, 0).wait_recv()
        for row in range(PAIR):
            w_vm[0, row] = v_vm[row].astype(BF16)
        hand(1, src_vm, 0).wait_recv()
        signs = [ahead(i) for i in range(ROWS)]

        def fine(i, carry):
            now = lax.rem(i, 2)
            later = 1 - now
            w = [w_vm[now, row] for row in range(ROWS)]
            inside = [
                dot(w[0], opt_vm[0, 0]) + dot(w[1], opt_vm[0, 2]),
                dot(w[0], opt_vm[1, 1]) + dot(w[1], opt_vm[1, 0]) + dot(w[2], opt_vm[1, 2]),
                dot(w[1], opt_vm[2, 1]) + dot(w[2], opt_vm[2, 0]) + dot(w[3], opt_vm[2, 2]),
                dot(w[2], opt_vm[3, 1]) + dot(w[3], opt_vm[3, 0]),
            ]

            @pl.when(i > 0)
            def _():
                for part in range(PARTS):
                    halo(later, 1, part).wait_send()

            @pl.when(i > 1)
            def _():
                for part in range(PARTS):
                    halo(later, 0, part).wait_send()

            for part in range(PARTS):
                at = slice(PART * part, PART * (part + 1))
                for side in range(2):
                    edge, next_in = (0, 1) if side == 0 else (3, 2)
                    toward = 1 + side

                    def update(row, change):
                        value = (v_vm[row, at] + change) + src_vm[row, at]
                        v_vm[row, at] = value
                        w_vm[later, row, at] = value.astype(BF16)

                    def send(what):
                        @pl.when(i < STEPS - 1)
                        def _():
                            halo(later, what, part).start()

                    halo_in(now, side, part).wait_recv()
                    near = halo_vm[now, side, their_side[side], at]
                    change = inside[edge][at] + dot(near, opt_vm[edge, toward])
                    far = halo_vm[now, side, 1 - their_side[side], at]
                    out = signs[edge] if side == 1 else jnp.logical_not(signs[edge])
                    update(edge, change + dot(jnp.where(out, far, w[3 - next_in][at]), opt_vm[edge, 3]))
                    out = signs[next_in] if side == 1 else jnp.logical_not(signs[next_in])
                    change = dot(jnp.where(out, near, w[3 - edge][at]), opt_vm[next_in, 3])
                    update(next_in, inside[next_in][at] + change)
                    send(side)

                    if side == 0 and part == PARTS - 1:

                        @pl.when(i == STEPS - 1)
                        def _():
                            hand(2, v_vm, 0).start()

            return carry

        lax.fori_loop(0, STEPS, fine, 0)
        for part in range(PARTS):
            for what in range(2):
                halo((STEPS - 1) % 2, what, part).wait_send()
        hand(2, v_vm, 0).wait_send()

    def send_out(chunk, last):
        for b in range(PAIR):
            ends = end_vm[b, CHUNK * chunk : CHUNK * (chunk + 1)] + last[b]
            for line in range(4):
                osend_vm[CHUNK * chunk : CHUNK * (chunk + 1), 4 * b + line, :] = ends[:, LANES * line : LANES * (line + 1)]

        def one(j, carry):
            to = CHUNK * chunk + lax.rem(inner + j, CHUNK)

            @pl.when(to != tm)
            def _():
                pltpu.make_async_remote_copy(
                    osend_vm.at[to], orecv_vm.at[q * 4 + tracer], a2a_sem.at[2], a2a_sem.at[3],
                    device_id=(to, s), device_id_type=MESH,
                ).start()

            return carry

        lax.fori_loop(0, CHUNK, one, 0)

    def result(b):
        at = b + flip * (1 - 2 * b)
        return jnp.where(core == 0, back_vm[at], v_vm[PAIR + at])

    scan([result(b) - end_vm[b] for b in range(PAIR)], send_out)
    orecv_vm[q * 4 + tracer] = osend_vm[tm]
    back = pltpu.make_async_remote_copy(
        osend_vm.at[pl.ds(0, 31)], orecv_vm.at[pl.ds(0, 31)], a2a_sem.at[2], a2a_sem.at[3],
        device_id=(tm, s), device_id_type=MESH,
    )
    back.wait_recv()
    for piece in range(8):
        for line in range(LINES):
            at = piece * PIECE + line * LANES
            out_ref[0, :, at : at + LANES] = orecv_vm[4 * piece : 4 * piece + 4, line, :]
    back.wait_send()
    all_pieces().wait_send()


def local(initial, sources, operator, col_blocks, coarse_inv):
    cells = initial.shape[1]
    cols = col_blocks.T
    return pl.pallas_call(
        kernel,
        out_shape=pltpu.VMEM((1, TRACERS, cells), F32),
        in_specs=[
            pl.BlockSpec(memory_space=pltpu.HBM),
            pl.BlockSpec(memory_space=pltpu.HBM),
            pl.BlockSpec(memory_space=pltpu.HBM),
            pl.BlockSpec(memory_space=pltpu.HBM),
            pl.BlockSpec(memory_space=pltpu.HBM),
        ],
        out_specs=pl.BlockSpec(memory_space=pltpu.VMEM),
        scratch_shapes=[
            pltpu.VMEM((TRACERS, cells), F32),
            pltpu.SMEM(cols.shape, jnp.int32),
            pltpu.VMEM((PAIR, BLK, BLK), F32),
            pltpu.VMEM((ROWS, 4, BLK, BLK), BF16),
            pltpu.VMEM((ROWS, 4, BLK, BLK), BF16),
            pltpu.VMEM((LEVELS, PAIR, BLK, BLK), BF16),
            pltpu.VMEM((LEVELS, PAIR, BLK, BLK), BF16),
            pltpu.VMEM((TRACERS, PIECE), F32),
            pltpu.VMEM((SLICES, LINES, LANES), F32),
            pltpu.VMEM((SLICES, LINES, LANES), F32),
            pltpu.VMEM((SLICES, LINES, LANES), F32),
            pltpu.VMEM((SLICES, LINES, LANES), F32),
            pltpu.VMEM((ROWS, SLICES, BLK), F32),
            pltpu.VMEM((ROWS, SLICES, BLK), F32),
            pltpu.VMEM((PAIR, SLICES, BLK), F32),
            pltpu.VMEM((PAIR, SLICES, BLK), F32),
            pltpu.VMEM((2, ROWS, SLICES, BLK), BF16),
            pltpu.VMEM((2, 2, PAIR, SLICES, BLK), BF16),
            pltpu.SemaphoreType.DMA((5,)),
            pltpu.SemaphoreType.DMA((4,)),
            pltpu.SemaphoreType.DMA((3, 2)),
            pltpu.SemaphoreType.DMA((2, 2, PARTS)),
            pltpu.SemaphoreType.DMA((2, 2, PARTS)),
        ],
        compiler_params=pltpu.CompilerParams(
            collective_id=0, has_side_effects=True, vmem_limit_bytes=63 << 20
        ),
        name="parareal",
    )(initial, sources, operator, cols, coarse_inv)


def solution(mesh):
    placed = (
        P(None, "space"),
        P("tm", None, "space"),
        P("space", None, None, None),
        P("space", None),
        P("space", None, None),
    )
    return jax.shard_map(
        local, mesh=mesh, in_specs=placed, out_specs=P("tm", None, "space"), check_vma=False
    )
```
